32 devices in a mesh: row: 4 (over y, x), col: 8 (over z, core).
Axes of the slice: x: 2, y: 2, z: 4, core: 2. Of those that a mesh axis runs over, the one named last changes fastest.
Arguments:
- tokens: bfloat16 [256, 10240], P('col', 'row'), may hold values from -6 to 6
- out_grad: bfloat16 [256, 10240], P('col', 'row'), may hold values from -3 to 3
- gate_weight: bfloat16 [10240, 26624], P('row', 'col'), may hold values from -0.0625 to 0.0625
- up_weight: bfloat16 [10240, 26624], P('row', 'col'), may hold values from -0.0625 to 0.0625
- down_weight: bfloat16 [26624, 10240], P('col', 'row'), may hold values from -0.0390625 to 0.0390625
- gate_mask: int32 [2560, 6656], P('row', 'col'), may hold values from 0 to 23
- up_mask: int32 [2560, 6656], P('row', 'col'), may hold values from 0 to 23
- down_mask: int32 [6656, 2560], P('col', 'row'), may hold values from 0 to 23
Outputs:
- input_grad: bfloat16 [256, 10240], P('col', 'row')
- gate_weight_grad: bfloat16 [10240, 26624], P('row', 'col')
- up_weight_grad: bfloat16 [10240, 26624], P('row', 'col')
- down_weight_grad: bfloat16 [26624, 10240], P('col', 'row')
The draws below stay inside these ranges and needn't reach their ends.
Inputs may be any that keep to these rules, and one draw needn't show every extreme that they name: `gate_mask`: each entry is a pattern code as the first step defines, so every row and every column of each 4 by 4 block of a pruned weight keeps exactly two entries. `up_mask`: as for gate_mask. `down_mask`: as for gate_mask.
All inputs are finite; a program needn't handle non-finite values.
Results may differ from the reference program's by a relative error of at most 0.0049.
Values may be sent and summed in bfloat16 or wider, within the bound.
No kernel may reach another device: no remote copies, remote signals or barrier semaphores. Data moves between devices by JAX's collectives and lax.ppermute only.
A program may use at most 256 MiB of HBM per device.

```python
import jax
import jax.numpy as jnp
from jax import lax

D = 10240
FF = 26624
TOKENS = 256


def set_ends(drawn, own_key, low, top_value):
    longest = drawn.shape.index(max(drawn.shape))
    spots = []
    for shift in (0, 1):
        where = [jax.random.randint(jax.random.fold_in(own_key, axis), (), 0, length) for axis, length in enumerate(drawn.shape)]
        where[longest] = (where[longest] + shift) % drawn.shape[longest]
        spots.append(tuple(where))
    return drawn.at[spots[0]].set(low).at[spots[1]].set(top_value)


def block_levels(rng, shape, split, smallest, high):
    level = 1.0
    for axis_at, blocks in split:
        heights = jax.random.uniform(jax.random.fold_in(jax.random.fold_in(rng, 6), axis_at), (blocks,), jnp.float32, smallest / len(split), high / len(split))
        level = level * jnp.repeat(jnp.exp(heights), shape[axis_at] // blocks).reshape((-1,) + (1,) * (len(shape) - 1 - axis_at))
    return level


def normal_values(stream_key, dims, scale, reach, split=(), kind=jnp.bfloat16):
    drawn = scale * jax.random.normal(stream_key, dims, jnp.float32)
    if split:
        drawn = drawn * block_levels(stream_key, dims, split, -0.22, 0.18)
    return jnp.clip(drawn, -reach, reach).astype(kind)


def setup_inputs(seed: int = 0) -> dict:
    splits = jax.random.split(jax.random.key(seed), 9)
    return {
        "tokens": normal_values(splits[0], (TOKENS, D), 1.0, 6.0, ((0, 8), (1, 4))),
        "out_grad": normal_values(splits[1], (TOKENS, D), 0.5, 3.0, ((0, 8), (1, 4))),
        "gate_weight": normal_values(splits[2], (D, FF), D ** -0.5, 0.0625, ((0, 4), (1, 8))),
        "up_weight": normal_values(splits[3], (D, FF), D ** -0.5, 0.0625, ((0, 4), (1, 8))),
        "down_weight": normal_values(splits[4], (FF, D), FF ** -0.5, 0.0390625, ((0, 8), (1, 4))),
        "gate_mask": set_ends(jax.random.randint(splits[5], (D // 4, FF // 4), 0, 24), jax.random.fold_in(splits[5], 1), 0, 23).astype(jnp.int32),
        "up_mask": set_ends(jax.random.randint(splits[6], (D // 4, FF // 4), 0, 24), jax.random.fold_in(splits[6], 1), 0, 23).astype(jnp.int32),
        "down_mask": set_ends(jax.random.randint(splits[7], (FF // 4, D // 4), 0, 24), jax.random.fold_in(splits[7], 1), 0, 23).astype(jnp.int32),
    }


def expand_mask(block_ids):
    lead_col = block_ids // 6
    second_rank = (block_ids // 2) % 3
    third_rank = block_ids % 2
    second_col = second_rank + (second_rank >= lead_col).astype(jnp.int32)
    low_col = jnp.minimum(lead_col, second_col)
    high_col = jnp.maximum(lead_col, second_col)
    rest_low = jnp.where(low_col > 0, 0, jnp.where(high_col > 1, 1, 2)).astype(jnp.int32)
    rest_high = 6 - low_col - high_col - rest_low
    third_col = jnp.where(third_rank == 0, rest_low, rest_high)
    fourth_col = 6 - lead_col - second_col - third_col
    ordering = jnp.stack([lead_col, second_col, third_col, fourth_col], axis=-1)
    next_cols = jnp.roll(ordering, -1, axis=-1)
    column_ids = jnp.arange(4, dtype=jnp.int32)
    chosen = (ordering[..., :, None] == column_ids) | (next_cols[..., :, None] == column_ids)
    group_rows, group_cols = block_ids.shape
    pattern = chosen.transpose(0, 2, 1, 3).reshape(4 * group_rows, 4 * group_cols)
    return pattern.astype(jnp.bfloat16)


def swiglu_back(gate_sum, up_sum, back_sum):
    logistic = jax.nn.sigmoid(gate_sum)
    swish_val = gate_sum * logistic
    hidden = (swish_val * up_sum).astype(jnp.bfloat16)
    up_grad = (back_sum * swish_val).astype(jnp.bfloat16)
    gate_grad = (back_sum * up_sum * logistic * (1.0 + gate_sum * (1.0 - logistic))).astype(jnp.bfloat16)
    return gate_grad, up_grad, hidden


def reference(tokens, out_grad, gate_weight, up_weight, down_weight, gate_mask, up_mask, down_mask):
    block_width = 2048 if FF % 2048 == 0 else FF
    block_count = FF // block_width
    gate_blocks = gate_weight.reshape(D, block_count, block_width).transpose(1, 0, 2)
    up_blocks = up_weight.reshape(D, block_count, block_width).transpose(1, 0, 2)
    down_blocks = down_weight.reshape(block_count, block_width, D)
    gate_codes = gate_mask.reshape(D // 4, block_count, block_width // 4).transpose(1, 0, 2)
    up_codes = up_mask.reshape(D // 4, block_count, block_width // 4).transpose(1, 0, 2)
    down_codes = down_mask.reshape(block_count, block_width // 4, D // 4)

    def one_block(input_acc, pieces):
        gate_w, up_w, down_w, gate_c, up_c, down_c = pieces
        gate_keep = expand_mask(gate_c)
        up_keep = expand_mask(up_c)
        down_keep = expand_mask(down_c)
        gate_pruned = gate_w * gate_keep
        up_pruned = up_w * up_keep
        down_pruned = down_w * down_keep
        gate_sum = jnp.dot(tokens, gate_pruned, preferred_element_type=jnp.float32)
        up_sum = jnp.dot(tokens, up_pruned, preferred_element_type=jnp.float32)
        back_sum = jnp.dot(out_grad, down_pruned.T, preferred_element_type=jnp.float32)
        gate_grad, up_grad, hidden = swiglu_back(gate_sum, up_sum, back_sum)
        input_acc = input_acc + jnp.dot(gate_grad, gate_pruned.T, preferred_element_type=jnp.float32)
        input_acc = input_acc + jnp.dot(up_grad, up_pruned.T, preferred_element_type=jnp.float32)
        gate_wg = (jnp.dot(tokens.T, gate_grad, preferred_element_type=jnp.float32) * gate_keep).astype(jnp.bfloat16)
        up_wg = (jnp.dot(tokens.T, up_grad, preferred_element_type=jnp.float32) * up_keep).astype(jnp.bfloat16)
        down_wg = (jnp.dot(hidden.T, out_grad, preferred_element_type=jnp.float32) * down_keep).astype(jnp.bfloat16)
        return input_acc, (gate_wg, up_wg, down_wg)

    start_acc = jnp.zeros((TOKENS, D), jnp.float32)
    input_acc, outputs = lax.scan(one_block, start_acc, (gate_blocks, up_blocks, down_blocks, gate_codes, up_codes, down_codes))
    gate_wg, up_wg, down_wg = outputs
    gate_weight_grad = gate_wg.transpose(1, 0, 2).reshape(D, FF)
    up_weight_grad = up_wg.transpose(1, 0, 2).reshape(D, FF)
    down_weight_grad = down_wg.reshape(FF, D)
    return input_acc.astype(jnp.bfloat16), gate_weight_grad, up_weight_grad, down_weight_grad
```

```python
import functools

import jax
import jax.numpy as jnp
from jax import lax
from jax.experimental import pallas as pl
from jax.experimental.pallas import tpu as pltpu
from jax.sharding import PartitionSpec as P

BF16 = jnp.bfloat16
F32 = jnp.float32
TILE = 256
PARTS = 4
VMEM = 52 * 2**20


def expand_mask(block_ids):
    lead_col = block_ids // 6
    second_rank = block_ids // 2 % 3
    third_rank = block_ids % 2
    second_col = second_rank + (second_rank >= lead_col).astype(jnp.int32)
    low_col = jnp.minimum(lead_col, second_col)
    high_col = jnp.maximum(lead_col, second_col)
    rest_low = jnp.where(low_col > 0, 0, jnp.where(high_col > 1, 1, 2)).astype(jnp.int32)
    rest_high = 6 - low_col - high_col - rest_low
    third_col = jnp.where(third_rank == 0, rest_low, rest_high)
    fourth_col = 6 - lead_col - second_col - third_col
    ordering = [lead_col, second_col, third_col, fourth_col]
    group_rows, group_cols = block_ids.shape
    col_position = lax.broadcasted_iota(jnp.int32, (group_rows, 4 * group_cols), 1) % 4
    row_list = []
    for local_row in range(4):
        current = jnp.repeat(ordering[local_row], 4, axis=1)
        following = jnp.repeat(ordering[(local_row + 1) % 4], 4, axis=1)
        row_list.append((current == col_position) | (following == col_position))
    pattern = jnp.stack(row_list, axis=1).reshape(4 * group_rows, 4 * group_cols)
    return pattern.astype(jnp.bfloat16)


def contract_last(left, right):
    return lax.dot_general(
        left, right, (((1,), (1,)), ((), ())), preferred_element_type=jnp.float32
    )


def contract_first(left, right):
    return lax.dot_general(
        left, right, (((0,), (0,)), ((), ())), preferred_element_type=jnp.float32
    )


def local_any(tokens, out_grad, gate_weight, up_weight, down_weight, gate_mask, up_mask, down_mask):
    gate_keep = expand_mask(gate_mask)
    up_keep = expand_mask(up_mask)
    down_keep = expand_mask(down_mask)
    gate_pruned = gate_weight * gate_keep
    up_pruned = up_weight * up_keep
    down_pruned = down_weight * down_keep
    panel_width = gate_pruned.shape[1]
    all_tokens, all_grads = (
        lax.all_gather(tokens, "col", axis=0, tiled=True),
        lax.all_gather(out_grad, "col", axis=0, tiled=True),
    )
    gate_sum = jnp.dot(all_tokens, gate_pruned, preferred_element_type=jnp.float32)
    up_sum = jnp.dot(all_tokens, up_pruned, preferred_element_type=jnp.float32)
    back_sum = contract_last(all_grads, down_pruned)
    shares = lax.psum_scatter(
        jnp.concatenate([gate_sum, up_sum, back_sum], axis=1),
        "row",
        scatter_dimension=0,
        tiled=True,
    )
    gate_sum = shares[:, :panel_width]
    up_sum = shares[:, panel_width : 2 * panel_width]
    back_sum = shares[:, 2 * panel_width :]
    logistic = jax.nn.sigmoid(gate_sum)
    swish_val = gate_sum * logistic
    hidden = swish_val * up_sum
    swiglu_up_grad = back_sum * swish_val
    swiglu_gate_grad = back_sum * up_sum * logistic * (1.0 + gate_sum * (1.0 - logistic))
    local_grads = jnp.concatenate([swiglu_gate_grad, swiglu_up_grad, hidden], axis=1).astype(
        jnp.bfloat16
    )
    all_local = lax.all_gather(local_grads, "row", axis=0, tiled=True)
    gate_grad = all_local[:, :panel_width]
    up_grad = all_local[:, panel_width : 2 * panel_width]
    hidden = all_local[:, 2 * panel_width :]
    input_grad = lax.psum_scatter(
        contract_last(gate_grad, gate_pruned) + contract_last(up_grad, up_pruned),
        "col",
        scatter_dimension=0,
        tiled=True,
    ).astype(jnp.bfloat16)
    gate_weight_grad = (contract_first(all_tokens, gate_grad) * gate_keep).astype(jnp.bfloat16)
    up_weight_grad = (contract_first(all_tokens, up_grad) * up_keep).astype(jnp.bfloat16)
    down_weight_grad = (contract_first(hidden, all_grads) * down_keep).astype(jnp.bfloat16)
    return (input_grad, gate_weight_grad, up_weight_grad, down_weight_grad)


def _nibble_words():
    table = []
    for code in range(24):
        rest = [0, 1, 2, 3]
        order = [rest.pop(code // 6), rest.pop(code // 2 % 3), rest.pop(code % 2), rest[0]]
        table.append([(1 << order[i]) | (1 << order[(i + 1) % 4]) for i in range(4)])
    words = []
    for i in range(4):
        row = []
        for third in range(3):
            word = sum(table[8 * third + k][i] << (4 * k) for k in range(8))
            row.append(word - (1 << 32) if word >= 1 << 31 else word)
        words.append(row)
    return words


NIBBLES = _nibble_words()


def _spread_rows(codes):
    low, mid = codes < 8, codes < 16
    shift = (codes & 7) * 4
    out = []
    for i in range(4):
        a, b, c = NIBBLES[i]
        word = jnp.where(low, jnp.int32(a), jnp.where(mid, jnp.int32(b), jnp.int32(c)))
        nibble = lax.shift_right_logical(word, shift) & 15
        out.append((nibble * 0x00204081) & 0x01010101)
    return out


def _interleave(words, lane_perm, row_perm):
    rows = words[0].shape[0]
    planes = [
        jnp.concatenate(
            [(lax.shift_right_logical(w, jnp.int32(8 * j)) & 255).astype(F32).astype(BF16) for j in range(4)], axis=1
        )
        for w in words
    ]
    wide = [jnp.dot(p, lane_perm, preferred_element_type=F32).astype(BF16) for p in planes]
    step = row_perm.shape[0] // 4
    out = []
    for at in range(0, rows, step):
        stacked = jnp.concatenate([w[at : at + step] for w in wide], axis=0)
        mixed = jnp.dot(row_perm, stacked, preferred_element_type=F32).astype(jnp.int32)
        out.append(jnp.where(mixed > 127, mixed - 256, mixed).astype(jnp.int8))
    return out


def _pack_rows_kernel(gate_ref, up_ref, lane_ref, row_ref, out_ref):
    rows = gate_ref.shape[0] // 4
    words = [None] * 4
    for s in range(8):
        ref, q = (gate_ref, s) if s < 4 else (up_ref, s - 4)
        spread = _spread_rows(ref[q * rows : (q + 1) * rows, :])
        for i in range(4):
            part = spread[i] << s if s else spread[i]
            words[i] = part if words[i] is None else words[i] | part
    at = 0
    for block in _interleave(words, lane_ref[...], row_ref[...]):
        out_ref[at : at + block.shape[0], :] = block
        at += block.shape[0]


def _pack_cols_kernel(groups, codes_ref, lane_ref, row_ref, out_ref):
    words = [None] * 4
    for q in range(groups):
        spread = _spread_rows(codes_ref[:, q * 128 : (q + 1) * 128])
        for i in range(4):
            part = spread[i] << q if q else spread[i]
            words[i] = part if words[i] is None else words[i] | part
    at = 0
    for block in _interleave(words, lane_ref[...], row_ref[...]):
        out_ref[at : at + block.shape[0], :] = block
        at += block.shape[0]


def _permutation(n):
    source = lax.broadcasted_iota(jnp.int32, (n, n), 0)
    target = lax.broadcasted_iota(jnp.int32, (n, n), 1)
    return (source == (target % 4) * (n // 4) + target // 4).astype(BF16)


def pack_masks(gate_mask, up_mask, down_mask):
    lanes = _permutation(512)
    code_rows, code_cols = gate_mask.shape
    row_perm = _permutation(128).T
    gate_up = pl.pallas_call(
        _pack_rows_kernel,
        grid=(pl.cdiv(code_cols, 128),),
        in_specs=[
            pl.BlockSpec((code_rows, 128), lambda j: (0, j)),
            pl.BlockSpec((code_rows, 128), lambda j: (0, j)),
            pl.BlockSpec((512, 512), lambda j: (0, 0)),
            pl.BlockSpec((128, 128), lambda j: (0, 0)),
        ],
        out_specs=pl.BlockSpec((code_rows, 512), lambda j: (0, j)),
        out_shape=jax.ShapeDtypeStruct((code_rows, 4 * code_cols), jnp.int8),
        compiler_params=pltpu.CompilerParams(vmem_limit_bytes=VMEM),
        cost_estimate=pl.CostEstimate(flops=3 * 10**9, bytes_accessed=10**7, transcendentals=0),
        name="pack_gate_up",
    )(gate_mask, up_mask, lanes, row_perm)
    down_rows, down_cols = down_mask.shape
    block = TILE // 4
    row_perm = _permutation(TILE).T
    down = pl.pallas_call(
        functools.partial(_pack_cols_kernel, down_cols // 128),
        grid=(down_rows // block,),
        in_specs=[
            pl.BlockSpec((block, down_cols), lambda j: (j, 0)),
            pl.BlockSpec((512, 512), lambda j: (0, 0)),
            pl.BlockSpec((TILE, TILE), lambda j: (0, 0)),
        ],
        out_specs=pl.BlockSpec((TILE, 512), lambda j: (j, 0)),
        out_shape=jax.ShapeDtypeStruct((4 * down_rows, 512), jnp.int8),
        compiler_params=pltpu.CompilerParams(vmem_limit_bytes=VMEM),
        cost_estimate=pl.CostEstimate(flops=2 * 10**9, bytes_accessed=5 * 10**6, transcendentals=0),
        name="pack_down",
    )(down_mask, lanes, row_perm)
    return gate_up, down


def _bit(packed, s):
    scale = -(2.0**-7) if s == 7 else 2.0**-s
    return (packed & jnp.int8(-128 if s == 7 else 1 << s)).astype(BF16) * BF16(scale)


def _rows_keep(packed, first):
    return jnp.concatenate([_bit(packed, first + q) for q in range(4)], axis=0)


def _cols_keep(packed, groups):
    return jnp.concatenate([_bit(packed, q) for q in range(groups)], axis=1)


def _store_sums(at, sums, own_ref, to_x_ref, to_y_ref, mix_ref):
    quarter = sums.shape[0] // 4
    half = quarter // 2
    cut = lambda k, n=1: sums[k * half : (k + n) * half]
    own_ref[at] = cut(0, 2)
    to_x_ref[at, :half] = cut(2).astype(BF16)
    to_x_ref[at, half:] = cut(6).astype(BF16)
    to_y_ref[at, :half] = cut(5).astype(BF16)
    to_y_ref[at, half:] = cut(7).astype(BF16)
    mix_ref[at] = cut(3, 2)


def _gate_up_kernel(tok_ref, gate_ref, up_ref, mask_ref, *out_refs):
    packed = mask_ref[...]
    tok = tok_ref[...]
    for at, ref in enumerate((gate_ref, up_ref)):
        pruned = ref[...] * _rows_keep(packed, 4 * at)
        _store_sums(at, jnp.dot(tok, pruned, preferred_element_type=F32), *out_refs)


def _back_kernel(grad_ref, down_ref, mask_ref, *out_refs):
    groups = down_ref.shape[1] // 512
    pruned = down_ref[...] * _cols_keep(mask_ref[...], groups)
    _store_sums(0, contract_last(grad_ref[...], pruned), *out_refs)


def _sum_outs(n, rows, width):
    quarter = rows // 4
    spec = pl.BlockSpec((n, quarter, TILE), lambda j: (0, 0, j))
    shape = lambda t: jax.ShapeDtypeStruct((n, quarter, width), t)
    return [spec] * 4, [shape(F32), shape(BF16), shape(BF16), shape(F32)]


def gate_up_sums(tok, gate_weight, up_weight, gate_up_bits, first, count):
    rows, depth = tok.shape
    specs, shapes = _sum_outs(2, rows, count * TILE)
    return pl.pallas_call(
        _gate_up_kernel,
        grid=(count,),
        in_specs=[
            pl.BlockSpec((rows, depth), lambda j: (0, 0)),
            pl.BlockSpec((depth, TILE), lambda j: (0, j + first)),
            pl.BlockSpec((depth, TILE), lambda j: (0, j + first)),
            pl.BlockSpec((depth // 4, TILE), lambda j: (0, j + first)),
        ],
        out_specs=specs,
        out_shape=shapes,
        compiler_params=pltpu.CompilerParams(vmem_limit_bytes=VMEM),
        cost_estimate=pl.CostEstimate(
            flops=4 * rows * depth * count * TILE, bytes_accessed=4 * depth * count * TILE, transcendentals=0
        ),
        name="gate_up_sums",
    )(tok, gate_weight, up_weight, gate_up_bits)


def back_sums(grads, down_weight, down_bits, first, count):
    rows, depth = grads.shape
    specs, shapes = _sum_outs(1, rows, count * TILE)
    return pl.pallas_call(
        _back_kernel,
        grid=(count,),
        in_specs=[
            pl.BlockSpec((rows, depth), lambda j: (0, 0)),
            pl.BlockSpec((TILE, depth), lambda j: (j + first, 0)),
            pl.BlockSpec((TILE, 512), lambda j: (j + first, 0)),
        ],
        out_specs=specs,
        out_shape=shapes,
        compiler_params=pltpu.CompilerParams(vmem_limit_bytes=VMEM),
        cost_estimate=pl.CostEstimate(
            flops=2 * rows * depth * count * TILE, bytes_accessed=2 * depth * count * TILE, transcendentals=0
        ),
        name="back_sums",
    )(grads, down_weight, down_bits)


def _swap(value, bit):
    return lax.ppermute(value, "row", [(i, i ^ bit) for i in range(4)])


def reduce_rows(sums):
    own, to_x, to_y, mix = sums
    half = own.shape[1] // 2
    from_x, from_y = _swap(to_x, 1), _swap(to_y, 2)
    mixed_x = (mix[:, :half] + from_y[:, half:]).astype(BF16)
    mixed_y = (mix[:, half:] + from_x[:, half:]).astype(BF16)
    second_x, second_y = _swap(mixed_x, 1), _swap(mixed_y, 2)
    first_half = own[:, :half] + from_x[:, :half] + second_y
    second_half = own[:, half:] + from_y[:, :half] + second_x
    return jnp.concatenate([first_half, second_half], axis=1)


def gather_rows(block):
    half = block.shape[1] // 2
    from_x, from_y = _swap(block, 1), _swap(block, 2)
    diag_a, diag_b = _swap(from_x[:, :half], 2), _swap(from_y[:, half:], 1)
    return block, from_x, from_y, diag_a, diag_b


def swiglu_back(gate_sum, up_sum, back_sum):
    logistic = jax.nn.sigmoid(gate_sum)
    swish_val = gate_sum * logistic
    hidden = swish_val * up_sum
    up_grad = back_sum * swish_val
    gate_grad = back_sum * up_sum * logistic * (1.0 + gate_sum * (1.0 - logistic))
    return jnp.stack([gate_grad, up_grad, hidden]).astype(BF16)


def _all_rows(refs, at):
    return jnp.concatenate([ref[at] for ref in refs], axis=0)


def _input_grad_part(block_refs, gate_ref, up_ref, gate_keep, up_keep):
    return contract_last(_all_rows(block_refs, 0), gate_ref[...] * gate_keep) + contract_last(
        _all_rows(block_refs, 1), up_ref[...] * up_keep
    )


def _weight_grads(tok_ref, grad_ref, block_refs, gate_keep, up_keep, down_keep, gate_out, up_out, down_out):
    tok = tok_ref[...]
    gate_out[...] = contract_first(tok, _all_rows(block_refs, 0)).astype(BF16) * gate_keep
    up_out[...] = contract_first(tok, _all_rows(block_refs, 1)).astype(BF16) * up_keep
    down_out[...] = contract_first(_all_rows(block_refs, 2), grad_ref[...]).astype(BF16) * down_keep


def _backward_kernel(with_acc, with_input, with_weights, n_alias, *refs):
    refs = list(refs)
    block_refs = [refs.pop(0) for _ in range(5)]
    bits = refs.pop(0)[...]
    gate_keep, up_keep = _rows_keep(bits, 0), _rows_keep(bits, 4)
    if with_input:
        gate_ref, up_ref = refs.pop(0), refs.pop(0)
        acc_ref = refs.pop(0) if with_acc else None
    if with_weights:
        tok_ref, grad_ref, down_bits = refs.pop(0), refs.pop(0), refs.pop(0)
        down_keep = _cols_keep(down_bits[...], grad_ref.shape[1] // 512)
        refs = refs[n_alias:]
    if with_input:
        sum_ref = refs.pop(0)
        part = _input_grad_part(block_refs, gate_ref, up_ref, gate_keep, up_keep)

        @pl.when(pl.program_id(0) == 0)
        def _():
            sum_ref[...] = part + acc_ref[...] if with_acc else part

        @pl.when(pl.program_id(0) > 0)
        def _():
            sum_ref[...] += part

    if with_weights:
        _weight_grads(tok_ref, grad_ref, block_refs, gate_keep, up_keep, down_keep, *refs)


def backward(blocks, gate_up_bits, first, count, inputs=None, weights=None):
    args, specs, out_specs, shapes, aliases = list(blocks), [], [], [], {}
    half = blocks[0].shape[1] // 2
    for block in blocks:
        specs.append(pl.BlockSpec((3, block.shape[1], TILE), lambda j: (0, 0, j)))
    rows = 8 * half
    depth = 4 * gate_up_bits.shape[0]
    width = gate_up_bits.shape[1]
    args.append(gate_up_bits)
    specs.append(pl.BlockSpec((depth // 4, TILE), lambda j: (0, j + first)))
    column_block = pl.BlockSpec((depth, TILE), lambda j: (0, j + first))
    whole = pl.BlockSpec((rows, depth), lambda j: (0, 0))
    flops = moved = 0
    if inputs is not None:
        gate_weight, up_weight, acc = inputs
        args += [gate_weight, up_weight]
        specs += [column_block, column_block]
        if acc is not None:
            args.append(acc)
            specs.append(whole)
        out_specs.append(whole)
        shapes.append(jax.ShapeDtypeStruct((rows, depth), F32))
        flops += 4 * rows * depth * count * TILE
        moved += 4 * depth * count * TILE
    n_alias = 0
    if weights is not None:
        tok, grads, down_bits, so_far = weights
        args += [tok, grads, down_bits]
        specs += [whole, whole, pl.BlockSpec((TILE, 512), lambda j: (j + first, 0))]
        if so_far is not None:
            n_alias = 3
            for k, value in enumerate(so_far):
                aliases[len(args)] = len(shapes) + k
                args.append(value)
                specs.append(pl.BlockSpec(memory_space=pl.ANY))
        out_specs += [column_block, column_block, pl.BlockSpec((TILE, depth), lambda j: (j + first, 0))]
        shapes += [jax.ShapeDtypeStruct((depth, width), BF16)] * 2 + [jax.ShapeDtypeStruct((width, depth), BF16)]
        flops += 6 * rows * depth * count * TILE
        moved += 6 * depth * count * TILE
    return pl.pallas_call(
        functools.partial(
            _backward_kernel, inputs is not None and inputs[2] is not None, inputs is not None, weights is not None, n_alias
        ),
        grid=(count,),
        in_specs=specs,
        out_specs=out_specs,
        out_shape=shapes,
        input_output_aliases=aliases,
        compiler_params=pltpu.CompilerParams(vmem_limit_bytes=VMEM),
        cost_estimate=pl.CostEstimate(flops=flops, bytes_accessed=moved, transcendentals=0),
        name="backward",
    )(*args)


def _col_swap(value, bits):
    return lax.ppermute(value, "col", [(i, i ^ bits) for i in range(8)])


def gather_tokens(value, order):
    mine = jnp.stack([value] + [_col_swap(value, 2 * k) for k in (1, 2, 3)])
    theirs = _col_swap(mine, 1)
    groups = []
    for p in range(4):
        for part in (mine, theirs):
            groups.append(lax.dynamic_index_in_dim(part, p ^ order, 0, keepdims=False))
    return jnp.concatenate(groups, axis=0)


def scatter_tokens(partial, order):
    depth = partial.shape[1]
    rows = partial.shape[0] // 8
    split = partial.reshape(4, 2, rows, depth)
    pair = split[:, 0] + _col_swap(split[:, 1], 1)
    total = lax.dynamic_index_in_dim(pair, order, 0, keepdims=False)
    for k in (1, 2, 3):
        sent = lax.dynamic_index_in_dim(pair, k ^ order, 0, keepdims=False).astype(BF16)
        total = total + _col_swap(sent, 2 * k)
    return total.astype(BF16)


def local_tiled(tokens, out_grad, gate_weight, up_weight, down_weight, gate_mask, up_mask, down_mask):
    order = lax.axis_index("row") ^ (lax.axis_index("col") // 2)
    tok = gather_tokens(tokens, order)
    gate_up_bits, down_bits = pack_masks(gate_mask, up_mask, down_mask)
    grads = gather_tokens(out_grad, order)
    tiles = gate_weight.shape[1] // TILE
    cuts = [tiles * k // PARTS for k in range(PARTS + 1)]
    chunks = [(a, b - a) for a, b in zip(cuts[:-1], cuts[1:])]
    blocks = []
    gate_up = [reduce_rows(gate_up_sums(tok, gate_weight, up_weight, gate_up_bits, *c)) for c in chunks]
    back = [reduce_rows(back_sums(grads, down_weight, down_bits, *c)) for c in chunks]
    for gu, b in zip(gate_up, back):
        blocks.append(gather_rows(swiglu_back(gu[0], gu[1], b[0])))
    acc, outs = None, None
    for k, c in enumerate(chunks):
        inputs = (gate_weight, up_weight, acc)
        weights = (tok, grads, down_bits, outs)
        if k < PARTS - 1:
            acc, *outs = backward(blocks[k], gate_up_bits, *c, inputs=inputs, weights=weights)
        else:
            (acc,) = backward(blocks[k], gate_up_bits, *c, inputs=inputs)
            outs = backward(blocks[k], gate_up_bits, *c, weights=weights)
    return (scatter_tokens(acc, order), *outs)


def tiled_fits(mesh, depth, width, token_rows):
    return (
        mesh.shape["row"] == 4
        and mesh.shape["col"] == 8
        and depth % 1280 == 0
        and depth // 512 <= 7
        and depth % 512 == 0
        and width % TILE == 0
        and width // TILE >= PARTS
        and token_rows % 256 == 0
    )


def solution(mesh):
    in_specs = (
        P("col", "row"),
        P("col", "row"),
        P("row", "col"),
        P("row", "col"),
        P("col", "row"),
        P("row", "col"),
        P("row", "col"),
        P("col", "row"),
    )
    out_specs = (P("col", "row"), P("row", "col"), P("row", "col"), P("col", "row"))

    def run(tokens, out_grad, gate_weight, *rest):
        depth = gate_weight.shape[0] // mesh.shape["row"]
        width = gate_weight.shape[1] // mesh.shape["col"]
        body = local_tiled if tiled_fits(mesh, depth, width, tokens.shape[0]) else local_any
        mapped = jax.shard_map(body, mesh=mesh, in_specs=in_specs, out_specs=out_specs, check_vma=False)
        return mapped(tokens, out_grad, gate_weight, *rest)

    return run
```

```python
import functools

import jax
import jax.numpy as jnp
from jax import lax
from jax.experimental import pallas as pl
from jax.experimental.pallas import tpu as pltpu
from jax.sharding import PartitionSpec as P

BF16 = jnp.bfloat16
F32 = jnp.float32
COST = pl.CostEstimate(flops=10**10, bytes_accessed=10**8, transcendentals=0)
TILE = 256
ANY = pl.BlockSpec(memory_space=pl.ANY)
HBM = pl.BlockSpec(memory_space=pltpu.HBM)
WHOLE = pl.BlockSpec(memory_space=pltpu.VMEM)
GATE_UP_CUTS = (6, 13)
BACK_CUTS = (6, 13)
GRAD_CUTS = (4, 8, 13)


def expand_mask(block_ids):
    lead_col = block_ids // 6
    second_rank = block_ids // 2 % 3
    third_rank = block_ids % 2
    second_col = second_rank + (second_rank >= lead_col).astype(jnp.int32)
    low_col = jnp.minimum(lead_col, second_col)
    high_col = jnp.maximum(lead_col, second_col)
    rest_low = jnp.where(low_col > 0, 0, jnp.where(high_col > 1, 1, 2)).astype(jnp.int32)
    rest_high = 6 - low_col - high_col - rest_low
    third_col = jnp.where(third_rank == 0, rest_low, rest_high)
    fourth_col = 6 - lead_col - second_col - third_col
    ordering = [lead_col, second_col, third_col, fourth_col]
    group_rows, group_cols = block_ids.shape
    col_position = lax.broadcasted_iota(jnp.int32, (group_rows, 4 * group_cols), 1) % 4
    row_list = []
    for local_row in range(4):
        current = jnp.repeat(ordering[local_row], 4, axis=1)
        following = jnp.repeat(ordering[(local_row + 1) % 4], 4, axis=1)
        row_list.append((current == col_position) | (following == col_position))
    pattern = jnp.stack(row_list, axis=1).reshape(4 * group_rows, 4 * group_cols)
    return pattern.astype(jnp.bfloat16)


def contract_last(left, right):
    return lax.dot_general(
        left, right, (((1,), (1,)), ((), ())), preferred_element_type=jnp.float32
    )


def contract_first(left, right):
    return lax.dot_general(
        left, right, (((0,), (0,)), ((), ())), preferred_element_type=jnp.float32
    )


def local_any(tokens, out_grad, gate_weight, up_weight, down_weight, gate_mask, up_mask, down_mask):
    gate_keep = expand_mask(gate_mask)
    up_keep = expand_mask(up_mask)
    down_keep = expand_mask(down_mask)
    gate_pruned = gate_weight * gate_keep
    up_pruned = up_weight * up_keep
    down_pruned = down_weight * down_keep
    panel_width = gate_pruned.shape[1]
    all_tokens, all_grads = (
        lax.all_gather(tokens, "col", axis=0, tiled=True),
        lax.all_gather(out_grad, "col", axis=0, tiled=True),
    )
    gate_sum = jnp.dot(all_tokens, gate_pruned, preferred_element_type=jnp.float32)
    up_sum = jnp.dot(all_tokens, up_pruned, preferred_element_type=jnp.float32)
    back_sum = contract_last(all_grads, down_pruned)
    shares = lax.psum_scatter(
        jnp.concatenate([gate_sum, up_sum, back_sum], axis=1),
        "row",
        scatter_dimension=0,
        tiled=True,
    )
    gate_sum = shares[:, :panel_width]
    up_sum = shares[:, panel_width : 2 * panel_width]
    back_sum = shares[:, 2 * panel_width :]
    logistic = jax.nn.sigmoid(gate_sum)
    swish_val = gate_sum * logistic
    hidden = swish_val * up_sum
    swiglu_up_grad = back_sum * swish_val
    swiglu_gate_grad = back_sum * up_sum * logistic * (1.0 + gate_sum * (1.0 - logistic))
    local_grads = jnp.concatenate([swiglu_gate_grad, swiglu_up_grad, hidden], axis=1).astype(
        jnp.bfloat16
    )
    all_local = lax.all_gather(local_grads, "row", axis=0, tiled=True)
    gate_grad = all_local[:, :panel_width]
    up_grad = all_local[:, panel_width : 2 * panel_width]
    hidden = all_local[:, 2 * panel_width :]
    input_grad = lax.psum_scatter(
        contract_last(gate_grad, gate_pruned) + contract_last(up_grad, up_pruned),
        "col",
        scatter_dimension=0,
        tiled=True,
    ).astype(jnp.bfloat16)
    gate_weight_grad = (contract_first(all_tokens, gate_grad) * gate_keep).astype(jnp.bfloat16)
    up_weight_grad = (contract_first(all_tokens, up_grad) * up_keep).astype(jnp.bfloat16)
    down_weight_grad = (contract_first(hidden, all_grads) * down_keep).astype(jnp.bfloat16)
    return (input_grad, gate_weight_grad, up_weight_grad, down_weight_grad)


def _spread_rows(codes):
    byte = lambda k: jnp.int32(1 << (8 * k))
    is0, is01, is012 = codes < 6, codes < 12, codes < 18
    first = jnp.where(is0, byte(0), jnp.where(is01, byte(1), jnp.where(is012, byte(2), byte(3))))
    rest = codes - jnp.where(is0, 0, jnp.where(is01, 6, jnp.where(is012, 12, 18)))
    low = jnp.where(is0, byte(1), byte(0))
    mid = jnp.where(is01, byte(2), byte(1))
    high = jnp.where(is012, byte(3), byte(2))
    early, late = rest < 2, rest < 4
    second = jnp.where(early, low, jnp.where(late, mid, high))
    third = jnp.where((rest & 1) == 0, jnp.where(early, mid, low), jnp.where(late, high, mid))
    return first | second, second | third


def _interleave(words, count, lane_perm, row_perm):
    rows = words[0].shape[0]
    wide = []
    for w in words:
        planes = [(lax.shift_right_logical(w, jnp.int32(8 * j)) & 255).astype(F32).astype(BF16) for j in range(4)]
        wide.append(jnp.dot(jnp.concatenate(planes, axis=1), lane_perm, preferred_element_type=F32).astype(BF16))
    step = row_perm.shape[0] // 4
    local_row = lax.broadcasted_iota(jnp.int32, (4 * step, 512), 0) % 4
    bias = 128 if count == 8 else 0
    base = jnp.where(local_row < 2, -bias, (1 << count) - 1 - bias)
    out = []
    for at in range(0, rows, step):
        stacked = jnp.concatenate([w[at : at + step] for w in wide], axis=0)
        mixed = jnp.dot(row_perm, stacked, preferred_element_type=F32).astype(jnp.int32)
        out.append((mixed + base).astype(jnp.int8))
    return out


def _words(pieces):
    words = None
    for s, codes in enumerate(pieces):
        part = [w << s if s else w for w in _spread_rows(codes)]
        words = part if words is None else [a | b for a, b in zip(words, part)]
    return words


def _pack_rows_kernel(gate_ref, up_ref, lane_ref, row_ref, out_ref):
    rows = gate_ref.shape[1] // 4
    pieces = []
    for ref in (gate_ref, up_ref):
        codes = ref[...].T
        pieces += [codes[q * rows : (q + 1) * rows, :] for q in range(4)]
    at = 0
    for block in _interleave(_words(pieces), len(pieces), lane_ref[...], row_ref[...]):
        out_ref[at : at + block.shape[0], :] = block
        at += block.shape[0]


def _pack_cols_kernel(codes_ref, lane_ref, row_ref, *refs):
    out_ref = refs[-1]
    block = row_ref.shape[0] // 4
    lanes, rows = lane_ref[...], row_ref[...]

    def step(t, carry):
        codes = codes_ref[pl.ds(pl.multiple_of(t * block, block), block), :]
        pieces = [codes[:, q : q + 128] for q in range(0, codes.shape[1], 128)]
        (packed,) = _interleave(_words(pieces), len(pieces), lanes, rows)
        out_ref[pl.ds(pl.multiple_of(t * 4 * block, 4 * block), 4 * block), :] = packed
        return carry

    lax.fori_loop(0, codes_ref.shape[0] // block, step, 0)


def _lane_permutation():
    source = lax.broadcasted_iota(jnp.int32, (512, 512), 0)
    target = lax.broadcasted_iota(jnp.int32, (512, 512), 1)
    return (source == (target % 4) * 128 + target // 4).astype(BF16)


def _row_permutation(n):
    target = lax.broadcasted_iota(jnp.int32, (4 * n, 2 * n), 0)
    source = lax.broadcasted_iota(jnp.int32, (4 * n, 2 * n), 1)
    hit = source == (target % 2) * n + target // 4
    return jnp.where(hit, jnp.where(target % 4 < 2, 1, -1), 0).astype(BF16)


def pack_gate_up(gate_mask, up_mask):
    code_rows, code_cols = gate_mask.shape
    return pl.pallas_call(
        _pack_rows_kernel,
        grid=(pl.cdiv(code_cols, 128),),
        in_specs=[
            pl.BlockSpec((128, code_rows), lambda j: (j, 0)),
            pl.BlockSpec((128, code_rows), lambda j: (j, 0)),
            pl.BlockSpec((512, 512), lambda j: (0, 0)),
            pl.BlockSpec((128, 64), lambda j: (0, 0)),
        ],
        out_specs=pl.BlockSpec((code_rows, 512), lambda j: (0, j)),
        out_shape=jax.ShapeDtypeStruct((code_rows, 4 * code_cols), jnp.int8),
        compiler_params=pltpu.CompilerParams(vmem_limit_bytes=46 * 2**20),
        cost_estimate=COST,
        name="pack_gate_up",
    )(gate_mask.T, up_mask.T, _lane_permutation(), _row_permutation(32))


def pack_down(down_mask, after):
    return pl.pallas_call(
        _pack_cols_kernel,
        in_specs=[WHOLE] * 3 + [ANY] * len(after),
        out_specs=WHOLE,
        out_shape=jax.ShapeDtypeStruct((4 * down_mask.shape[0], 512), jnp.int8),
        compiler_params=pltpu.CompilerParams(vmem_limit_bytes=46 * 2**20),
        cost_estimate=COST,
        name="pack_down",
    )(down_mask, _lane_permutation(), _row_permutation(TILE // 4), *after)


def _bit(packed, s):
    if s == 7:
        return BF16(1) + (packed & jnp.int8(-128)).astype(BF16) * BF16(2.0**-7)
    return (packed & jnp.int8(1 << s)).astype(BF16) * BF16(2.0**-s)


def _rows_keep(packed, first):
    return jnp.concatenate([_bit(packed, first + q) for q in range(4)], axis=0)


def _cols_keep(packed, groups):
    return jnp.concatenate([_bit(packed, q) for q in range(groups)], axis=1)


def _tile(t):
    return pl.ds(pl.multiple_of(t * TILE, TILE), TILE)


class _Loads:
    def __init__(self, panels, bufs, sems, first, count):
        self.panels, self.bufs, self.sems, self.first, self.count = panels, bufs, sems, first, count

    def copy(self, k, t):
        panel, by_rows = self.panels[k]
        at = pl.ds(pl.multiple_of((self.first + t) * TILE, TILE), TILE)
        source = panel.at[at, :] if by_rows else panel.at[:, at]
        return pltpu.make_async_copy(source, self.bufs[k].at[t], self.sems.at[k, t])

    def start(self):
        for t in range(self.count):
            for k in range(len(self.panels)):
                self.copy(k, t).start()

    def copy_out(self, k, t):
        panel, by_rows = self.panels[k]
        at = pl.ds(pl.multiple_of((self.first + t) * TILE, TILE), TILE)
        target = panel.at[at, :] if by_rows else panel.at[:, at]
        return pltpu.make_async_copy(self.bufs[k].at[t], target, self.sems.at[k, t])

    def wait_out(self):
        for t in range(self.count):
            for k in range(len(self.panels)):
                self.copy_out(k, t).wait()

    def wait(self, t):
        for k in range(len(self.panels)):
            self.copy(k, t).wait()


def _load_scratch(panels, count):
    shapes = []
    for panel, by_rows in panels:
        block = (TILE, panel.shape[1]) if by_rows else (panel.shape[0], TILE)
        shapes.append(pltpu.VMEM((count, *block), panel.dtype))
    return shapes, pltpu.SemaphoreType.DMA((len(panels), count))


def _store_sums(at, t, sums, own_ref, to_x_ref, to_y_ref, mix_ref):
    half = sums.shape[0] // 8
    cut = lambda k, n=1: sums[k * half : (k + n) * half]
    lanes = _tile(t)
    own_ref[at, :, lanes] = cut(0, 2)
    to_x_ref[at, :half, lanes] = cut(2).astype(BF16)
    to_x_ref[at, half:, lanes] = cut(6).astype(BF16)
    to_y_ref[at, :half, lanes] = cut(5).astype(BF16)
    to_y_ref[at, half:, lanes] = cut(7).astype(BF16)
    mix_ref[at, :, lanes] = cut(3, 2)


def _gate_up_kernel(first, count, n_after, tok_ref, gate_any, up_any, bits_any, *refs):
    out_refs, (gate_buf, up_buf, bits_buf, sems) = refs[n_after : n_after + 4], refs[n_after + 4 :]
    loads = _Loads(
        [(gate_any, False), (up_any, False), (bits_any, False)], (gate_buf, up_buf, bits_buf), sems, first, count
    )
    loads.start()

    def step(t, carry):
        loads.wait(t)
        packed = bits_buf[t]
        for at, buf in enumerate((gate_buf, up_buf)):
            pruned = buf[t] * _rows_keep(packed, 4 * at)
            _store_sums(at, t, jnp.dot(tok_ref[...], pruned, preferred_element_type=F32), *out_refs)
        return carry

    lax.fori_loop(0, count, step, 0)


def _back_kernel(first, count, n_after, grad_ref, down_any, bits_any, *refs):
    out_refs, (down_buf, bits_buf, sems) = refs[n_after : n_after + 4], refs[n_after + 4 :]
    loads = _Loads([(down_any, True), (bits_any, True)], (down_buf, bits_buf), sems, first, count)
    loads.start()
    groups = grad_ref.shape[1] // 512

    def step(t, carry):
        loads.wait(t)
        pruned = down_buf[t] * _cols_keep(bits_buf[t], groups)
        _store_sums(0, t, contract_last(grad_ref[...], pruned), *out_refs)
        return carry

    lax.fori_loop(0, count, step, 0)


def _sum_shapes(n, rows, width):
    shape = lambda t: jax.ShapeDtypeStruct((n, rows // 4, width), t)
    return [shape(F32), shape(BF16), shape(BF16), shape(F32)]


def gate_up_sums(tok, gate_weight, up_weight, gate_up_bits, first, count, after=()):
    rows, depth = tok.shape
    bufs, sems = _load_scratch([(gate_weight, False), (up_weight, False), (gate_up_bits, False)], count)
    return pl.pallas_call(
        functools.partial(_gate_up_kernel, first, count, len(after)),
        in_specs=[WHOLE, HBM, HBM, HBM] + [ANY] * len(after),
        out_specs=[WHOLE] * 4,
        out_shape=_sum_shapes(2, rows, count * TILE),
        scratch_shapes=[*bufs, sems],
        compiler_params=pltpu.CompilerParams(vmem_limit_bytes=46 * 2**20),
        cost_estimate=COST,
        name="gate_up_sums",
    )(tok, gate_weight, up_weight, gate_up_bits, *after)


def back_sums(grads, down_weight, down_bits, first, count, after=()):
    rows, depth = grads.shape
    bufs, sems = _load_scratch([(down_weight, True), (down_bits, True)], count)
    return pl.pallas_call(
        functools.partial(_back_kernel, first, count, len(after)),
        in_specs=[WHOLE, HBM, HBM] + [ANY] * len(after),
        out_specs=[WHOLE] * 4,
        out_shape=_sum_shapes(1, rows, count * TILE),
        scratch_shapes=[*bufs, sems],
        compiler_params=pltpu.CompilerParams(vmem_limit_bytes=46 * 2**20),
        cost_estimate=COST,
        name="back_sums",
    )(grads, down_weight, down_bits, *after)


def _swap(value, bit):
    return lax.ppermute(value, "row", [(i, i ^ bit) for i in range(4)])


def _widen(parts):
    return jnp.concatenate(parts, axis=2) if len(parts) > 1 else parts[0]


class Reduction:
    def __init__(self):
        self.sums, self.received = [], []

    def first(self, sums):
        _, to_x, to_y, _ = sums
        self.sums.append(sums)
        self.received.append((_swap(to_x, 1), _swap(to_y, 2)))

    def mixed(self):
        half = self.sums[0][0].shape[1] // 2
        pairs = list(zip(self.sums, self.received))
        self.mixed_x = _widen([(s[3][:, :half] + r[1][:, half:]).astype(BF16) for s, r in pairs])
        self.mixed_y = _widen([(s[3][:, half:] + r[0][:, half:]).astype(BF16) for s, r in pairs])

    def second(self):
        self.second_x, self.second_y = _swap(self.mixed_x, 1), _swap(self.mixed_y, 2)

    def hold_first(self, until):
        self.received[-1] = _hold(self.received[-1], until)

    def hold_second(self, until):
        self.second_x, self.second_y = _hold((self.second_x, self.second_y), until)

    def total(self):
        half = self.sums[0][0].shape[1] // 2
        pairs = list(zip(self.sums, self.received))
        first_half = _widen([s[0][:, :half] + r[0][:, :half] for s, r in pairs]) + self.second_y
        second_half = _widen([s[0][:, half:] + r[1][:, :half] for s, r in pairs]) + self.second_x
        return jnp.concatenate([first_half, second_half], axis=1)


def _hold(values, until):
    return lax.optimization_barrier((values, until))[0]


class Gathering:
    def __init__(self, block):
        self.block = block

    def first(self):
        self.from_x, self.from_y = _swap(self.block, 1), _swap(self.block, 2)

    def hold_first(self, until):
        self.from_x, self.from_y = _hold((self.from_x, self.from_y), until)

    def cut(self):
        half = self.block.shape[1] // 2
        self.cut_x, self.cut_y = self.from_x[:, :half], self.from_y[:, half:]

    def second(self):
        diag_a, diag_b = _swap(self.cut_x, 2), _swap(self.cut_y, 1)
        self.blocks = (self.block, self.from_x, self.from_y, diag_a, diag_b)


def swiglu(gate_sum, up_sum):
    return (gate_sum * jax.nn.sigmoid(gate_sum) * up_sum).astype(BF16)


def swiglu_back(gate_sum, up_sum, back_sum):
    logistic = jax.nn.sigmoid(gate_sum)
    up_grad = back_sum * (gate_sum * logistic)
    gate_grad = back_sum * up_sum * logistic * (1.0 + gate_sum * (1.0 - logistic))
    return jnp.stack([gate_grad, up_grad]).astype(BF16)


def _backward_kernel(first, count, with_acc, with_input, with_weights, n_alias, n_after, *refs):
    refs = list(refs)
    take = lambda n: [refs.pop(0) for _ in range(n)]
    block_refs = take(5)
    panels = [(ref, False) for ref in take(1)]
    if with_input:
        panels += [(ref, False) for ref in take(2)]
        acc_refs = take(2) if with_acc else []
    if with_weights:
        (tok_ref,) = take(1)
        take(n_alias)
    take(n_after)
    sum_refs = take(2) if with_input else []
    outs = take(2) if with_weights else []
    bufs = take(len(panels))
    out_bufs = take(2) if with_weights else []
    load_sems = refs.pop(0)
    loads = _Loads(panels, bufs, load_sems, first, count)
    stores = _Loads([(ref, False) for ref in outs], out_bufs, refs.pop(0), first, count) if with_weights else None
    loads.start()
    if with_input:
        for k, ref in enumerate(sum_refs):
            ref[...] = acc_refs[k][...] if with_acc else jnp.zeros_like(ref)

    def step(t, carry):
        loads.wait(t)
        lanes = _tile(t)
        rows_of = lambda k: jnp.concatenate([ref[k, :, lanes] for ref in block_refs], axis=0)
        packed = bufs[0][t]
        gate_keep, up_keep = _rows_keep(packed, 0), _rows_keep(packed, 4)
        gate_grad, up_grad = rows_of(0), rows_of(1)
        if with_weights:
            tok = tok_ref[...]
            out_bufs[0][t] = contract_first(tok, gate_grad).astype(BF16) * gate_keep
            stores.copy_out(0, t).start()
            out_bufs[1][t] = contract_first(tok, up_grad).astype(BF16) * up_keep
            stores.copy_out(1, t).start()
        if with_input:
            part = contract_last(gate_grad, bufs[1][t] * gate_keep) + contract_last(up_grad, bufs[2][t] * up_keep)
            half = sum_refs[0].shape[1]
            for p in range(4):
                for k, ref in enumerate(sum_refs):
                    ref[p] += part[(2 * p + k) * half : (2 * p + k + 1) * half]
        return carry

    lax.fori_loop(0, count, step, 0)
    if with_weights:
        stores.wait_out()


def backward(blocks, gate_up_bits, first, count, inputs=None, weights=None, after=()):
    args, specs, shapes, out_specs, aliases = list(blocks), [WHOLE] * 5, [], [], {}
    rows = 4 * blocks[0].shape[1]
    depth = 4 * gate_up_bits.shape[0]
    width = gate_up_bits.shape[1]
    panels, outs = [(gate_up_bits, False)], []
    args.append(gate_up_bits)
    specs.append(HBM)
    if inputs is not None:
        gate_weight, up_weight, acc = inputs
        panels += [(gate_weight, False), (up_weight, False)]
        args += [gate_weight, up_weight]
        specs += [HBM, HBM]
        if acc is not None:
            args += acc
            specs += [WHOLE] * 2
        shapes += [jax.ShapeDtypeStruct((4, rows // 8, depth), F32)] * 2
        out_specs += [WHOLE] * 2
    n_alias = 0
    if weights is not None:
        tok, so_far = weights
        args.append(tok)
        specs.append(WHOLE)
        if so_far is not None:
            n_alias = 2
            for k, value in enumerate(so_far):
                aliases[len(args)] = len(shapes) + k
                args.append(value)
                specs.append(HBM)
        outs = [jax.ShapeDtypeStruct((depth, width), BF16)] * 2
        shapes += outs
        out_specs += [HBM] * 2
    bufs, sems = _load_scratch(panels, count)
    scratch = [*bufs, sems]
    if weights is not None:
        out_bufs, out_sems = _load_scratch([(out, False) for out in outs], count)
        scratch = [*bufs, *out_bufs, sems, out_sems]
    args += list(after)
    specs += [ANY] * len(after)
    return pl.pallas_call(
        functools.partial(
            _backward_kernel,
            first,
            count,
            inputs is not None and inputs[2] is not None,
            inputs is not None,
            weights is not None,
            n_alias,
            len(after),
        ),
        in_specs=specs,
        out_specs=out_specs,
        out_shape=shapes,
        scratch_shapes=scratch,
        input_output_aliases=aliases,
        compiler_params=pltpu.CompilerParams(vmem_limit_bytes=46 * 2**20),
        cost_estimate=COST,
        name="backward",
    )(*args)


def _down_grad_kernel(count, n_after, *refs):
    block_refs, (grad_ref, bits_any), (out_any, bits_buf, out_buf, sems, out_sems) = refs[:5], refs[5:7], refs[7 + n_after :]
    loads = _Loads([(bits_any, True)], [bits_buf], sems, 0, count)
    stores = _Loads([(out_any, True)], [out_buf], out_sems, 0, count)
    loads.start()

    def step(t, carry):
        loads.wait(t)
        hidden = jnp.concatenate([ref[0, :, _tile(t)] for ref in block_refs], axis=0)
        keep = _cols_keep(bits_buf[t], grad_ref.shape[1] // 512)
        out_buf[t] = contract_first(hidden, grad_ref[...]).astype(BF16) * keep
        stores.copy_out(0, t).start()
        return carry

    lax.fori_loop(0, count, step, 0)
    stores.wait_out()


def down_grad(blocks, grads, down_bits, after=()):
    width, depth = down_bits.shape[0], grads.shape[1]
    count = width // TILE
    out = jax.ShapeDtypeStruct((width, depth), BF16)
    (bits_buf,), sems = _load_scratch([(down_bits, True)], count)
    (out_buf,), out_sems = _load_scratch([(out, True)], count)
    return pl.pallas_call(
        functools.partial(_down_grad_kernel, count, len(after)),
        in_specs=[WHOLE] * 6 + [HBM] + [ANY] * len(after),
        out_specs=HBM,
        out_shape=out,
        scratch_shapes=[bits_buf, out_buf, sems, out_sems],
        compiler_params=pltpu.CompilerParams(vmem_limit_bytes=46 * 2**20),
        cost_estimate=COST,
        name="down_grad",
    )(*blocks, grads, down_bits, *after)


def _col_swap(value, bits):
    return lax.ppermute(value, "col", [(i, i ^ bits) for i in range(8)])


def gather_groups(value):
    return [value] + [_col_swap(value, 2 * k) for k in (1, 2, 3)]


def order_groups(mine, theirs, order):
    groups = []
    for p in range(4):
        for part in (mine, theirs):
            groups.append(lax.dynamic_index_in_dim(part, p ^ order, 0, keepdims=False))
    return jnp.concatenate(groups, axis=0)


def chunks_of(tiles, cuts):
    ends = [0] + [(tiles * c + 6) // 13 for c in cuts]
    return [(a, b - a) for a, b in zip(ends[:-1], ends[1:])]


def local_tiled(tokens, out_grad, gate_weight, up_weight, down_weight, gate_mask, up_mask, down_mask):
    order = lax.axis_index("row") ^ (lax.axis_index("col") // 2)
    tiles = gate_weight.shape[1] // TILE
    gate_up_bits = pack_gate_up(gate_mask, up_mask)
    tok_mine, gate_up_bits = lax.optimization_barrier((gather_groups(tokens), gate_up_bits))
    tok_mine = jnp.stack(tok_mine)
    tok_theirs = _col_swap(tok_mine, 1)
    tok = order_groups(tok_mine, tok_theirs, order)
    gate_up = lambda c, after: gate_up_sums(tok, gate_weight, up_weight, gate_up_bits, *c, after=after)
    back = lambda c, after: back_sums(grads, down_weight, down_bits, *c, after=after)
    gate_up_red, back_red = Reduction(), Reduction()

    cuts = chunks_of(tiles, GATE_UP_CUTS)
    sums0 = gate_up(cuts[0], [])
    gate_up_red.first(sums0)
    sums1 = gate_up(cuts[1], [sums0[0]])
    gate_up_red.hold_first(sums1[0])
    gate_up_red.first(sums1)
    grad_mine = gather_groups(_hold(out_grad, sums1[0]))
    down_bits = pack_down(down_mask, [sums1[0], *gate_up_red.received[0]])
    gate_up_red.hold_first(down_bits)
    grad_mine = jnp.stack(_hold(grad_mine, down_bits))
    grad_theirs = _col_swap(grad_mine, 1)
    gate_up_red.mixed()
    gate_up_red.second()
    grads = order_groups(grad_mine, grad_theirs, order)
    cuts = chunks_of(tiles, BACK_CUTS)
    sums0 = back(cuts[0], [gate_up_red.mixed_x, gate_up_red.mixed_y])
    back_red.first(sums0)
    sums1 = back(cuts[1], [sums0[0]])
    back_red.hold_first(sums1[0])
    gate_up_red.hold_second(sums1[0])
    back_red.first(sums1)
    gate_up_total = gate_up_red.total()
    hidden = Gathering(swiglu(*gate_up_total)[None])
    gate_up_total = _hold(gate_up_total, hidden.block)
    hidden.first()
    hidden.cut()
    hidden.second()
    back_red.mixed()
    back_red.second()
    block = swiglu_back(*gate_up_total, *back_red.total())
    chunks = chunks_of(tiles, GRAD_CUTS)
    gath = [Gathering(block[:, :, a * TILE : (a + n) * TILE]) for a, n in chunks]
    gath[0].first()
    gath[1].first()
    down_out = down_grad(hidden.blocks, grads, down_bits, [gath[0].block, gath[1].block])
    gath[0].hold_first(down_out)
    gath[1].hold_first(down_out)
    gath[0].cut()
    gath[0].second()
    gath[1].cut()
    gath[1].second()
    gath[2].block = _hold(gath[2].block, down_out)
    gath[2].first()
    pair = (gate_weight, up_weight)
    acc = backward(gath[0].blocks, gate_up_bits, *chunks[0], inputs=(*pair, None), after=[gath[1].cut_x, gath[1].cut_y])
    gath[2].hold_first(acc[0])
    gath[2].cut()
    gath[2].second()
    acc = backward(gath[1].blocks, gate_up_bits, *chunks[1], inputs=(*pair, acc), after=[gath[2].cut_x, gath[2].cut_y])
    acc = backward(gath[2].blocks, gate_up_bits, *chunks[2], inputs=(*pair, acc))
    pairs = acc[0] + _col_swap(acc[1], 1)
    own = lax.dynamic_index_in_dim(pairs, order, 0, keepdims=False)
    sent = [lax.dynamic_index_in_dim(pairs, k ^ order, 0, keepdims=False).astype(BF16) for k in (1, 2, 3)]
    received = [_col_swap(value, 2 * k) for k, value in zip((1, 2, 3), sent)]
    outs = backward(gath[0].blocks, gate_up_bits, *chunks[0], weights=(tok, None), after=sent)
    outs = backward(gath[1].blocks, gate_up_bits, *chunks[1], weights=(tok, outs))
    outs = backward(gath[2].blocks, gate_up_bits, *chunks[2], weights=(tok, outs))
    for value in received:
        own = own + value
    return (own.astype(BF16), *outs, down_out)


def tiled_fits(mesh, depth, width, token_rows):
    return (
        mesh.shape["row"] == 4
        and mesh.shape["col"] == 8
        and depth % 1280 == 0
        and depth // 512 <= 7
        and depth % 512 == 0
        and width % TILE == 0
        and width // TILE >= 13
        and token_rows % 256 == 0
    )


def solution(mesh):
    in_specs = (
        P("col", "row"),
        P("col", "row"),
        P("row", "col"),
        P("row", "col"),
        P("col", "row"),
        P("row", "col"),
        P("row", "col"),
        P("col", "row"),
    )
    out_specs = (P("col", "row"), P("row", "col"), P("row", "col"), P("col", "row"))

    def run(tokens, out_grad, gate_weight, *rest):
        depth = gate_weight.shape[0] // mesh.shape["row"]
        width = gate_weight.shape[1] // mesh.shape["col"]
        body = local_tiled if tiled_fits(mesh, depth, width, tokens.shape[0]) else local_any
        mapped = jax.shard_map(body, mesh=mesh, in_specs=in_specs, out_specs=out_specs, check_vma=False)
        return mapped(tokens, out_grad, gate_weight, *rest)

    return run
```

```python
import functools

import jax
import jax.numpy as jnp
from jax import lax
from jax.experimental import pallas as pl
from jax.experimental.pallas import tpu as pltpu
from jax.sharding import PartitionSpec as P

BF16 = jnp.bfloat16
F32 = jnp.float32
COST = pl.CostEstimate(flops=10**10, bytes_accessed=10**8, transcendentals=0)
TILE = 256
ANY = pl.BlockSpec(memory_space=pl.ANY)
HBM = pl.BlockSpec(memory_space=pltpu.HBM)
WHOLE = pl.BlockSpec(memory_space=pltpu.VMEM)
GATE_UP_CUTS = (6, 13)
BACK_CUTS = (4, 13)


def expand_mask(block_ids):
    lead_col = block_ids // 6
    second_rank = block_ids // 2 % 3
    third_rank = block_ids % 2
    second_col = second_rank + (second_rank >= lead_col).astype(jnp.int32)
    low_col = jnp.minimum(lead_col, second_col)
    high_col = jnp.maximum(lead_col, second_col)
    rest_low = jnp.where(low_col > 0, 0, jnp.where(high_col > 1, 1, 2)).astype(jnp.int32)
    rest_high = 6 - low_col - high_col - rest_low
    third_col = jnp.where(third_rank == 0, rest_low, rest_high)
    fourth_col = 6 - lead_col - second_col - third_col
    ordering = [lead_col, second_col, third_col, fourth_col]
    group_rows, group_cols = block_ids.shape
    col_position = lax.broadcasted_iota(jnp.int32, (group_rows, 4 * group_cols), 1) % 4
    row_list = []
    for local_row in range(4):
        current = jnp.repeat(ordering[local_row], 4, axis=1)
        following = jnp.repeat(ordering[(local_row + 1) % 4], 4, axis=1)
        row_list.append((current == col_position) | (following == col_position))
    pattern = jnp.stack(row_list, axis=1).reshape(4 * group_rows, 4 * group_cols)
    return pattern.astype(jnp.bfloat16)


def contract_last(left, right):
    return lax.dot_general(
        left, right, (((1,), (1,)), ((), ())), preferred_element_type=jnp.float32
    )


def contract_first(left, right):
    return lax.dot_general(
        left, right, (((0,), (0,)), ((), ())), preferred_element_type=jnp.float32
    )


def local_any(tokens, out_grad, gate_weight, up_weight, down_weight, gate_mask, up_mask, down_mask):
    gate_keep = expand_mask(gate_mask)
    up_keep = expand_mask(up_mask)
    down_keep = expand_mask(down_mask)
    gate_pruned = gate_weight * gate_keep
    up_pruned = up_weight * up_keep
    down_pruned = down_weight * down_keep
    panel_width = gate_pruned.shape[1]
    all_tokens, all_grads = (
        lax.all_gather(tokens, "col", axis=0, tiled=True),
        lax.all_gather(out_grad, "col", axis=0, tiled=True),
    )
    gate_sum = jnp.dot(all_tokens, gate_pruned, preferred_element_type=jnp.float32)
    up_sum = jnp.dot(all_tokens, up_pruned, preferred_element_type=jnp.float32)
    back_sum = contract_last(all_grads, down_pruned)
    shares = lax.psum_scatter(
        jnp.concatenate([gate_sum, up_sum, back_sum], axis=1),
        "row",
        scatter_dimension=0,
        tiled=True,
    )
    gate_sum = shares[:, :panel_width]
    up_sum = shares[:, panel_width : 2 * panel_width]
    back_sum = shares[:, 2 * panel_width :]
    logistic = jax.nn.sigmoid(gate_sum)
    swish_val = gate_sum * logistic
    hidden = swish_val * up_sum
    swiglu_up_grad = back_sum * swish_val
    swiglu_gate_grad = back_sum * up_sum * logistic * (1.0 + gate_sum * (1.0 - logistic))
    local_grads = jnp.concatenate([swiglu_gate_grad, swiglu_up_grad, hidden], axis=1).astype(
        jnp.bfloat16
    )
    all_local = lax.all_gather(local_grads, "row", axis=0, tiled=True)
    gate_grad = all_local[:, :panel_width]
    up_grad = all_local[:, panel_width : 2 * panel_width]
    hidden = all_local[:, 2 * panel_width :]
    input_grad = lax.psum_scatter(
        contract_last(gate_grad, gate_pruned) + contract_last(up_grad, up_pruned),
        "col",
        scatter_dimension=0,
        tiled=True,
    ).astype(jnp.bfloat16)
    gate_weight_grad = (contract_first(all_tokens, gate_grad) * gate_keep).astype(jnp.bfloat16)
    up_weight_grad = (contract_first(all_tokens, up_grad) * up_keep).astype(jnp.bfloat16)
    down_weight_grad = (contract_first(hidden, all_grads) * down_keep).astype(jnp.bfloat16)
    return (input_grad, gate_weight_grad, up_weight_grad, down_weight_grad)


def _spread_rows(codes):
    byte = lambda k: jnp.int32(1 << (8 * k))
    is0, is01, is012 = codes < 6, codes < 12, codes < 18
    first = jnp.where(is0, byte(0), jnp.where(is01, byte(1), jnp.where(is012, byte(2), byte(3))))
    rest = codes - jnp.where(is0, 0, jnp.where(is01, 6, jnp.where(is012, 12, 18)))
    low = jnp.where(is0, byte(1), byte(0))
    mid = jnp.where(is01, byte(2), byte(1))
    high = jnp.where(is012, byte(3), byte(2))
    early, late = rest < 2, rest < 4
    second = jnp.where(early, low, jnp.where(late, mid, high))
    third = jnp.where((rest & 1) == 0, jnp.where(early, mid, low), jnp.where(late, high, mid))
    return first | second, second | third


def _interleave(words, count, lane_perm, row_perm):
    rows = words[0].shape[0]
    wide = []
    for w in words:
        planes = [(lax.shift_right_logical(w, jnp.int32(8 * j)) & 255).astype(F32).astype(BF16) for j in range(4)]
        wide.append(jnp.dot(jnp.concatenate(planes, axis=1), lane_perm, preferred_element_type=F32).astype(BF16))
    step = row_perm.shape[0] // 4
    local_row = lax.broadcasted_iota(jnp.int32, (4 * step, 512), 0) % 4
    bias = 128 if count == 8 else 0
    base = jnp.where(local_row < 2, -bias, (1 << count) - 1 - bias)
    out = []
    for at in range(0, rows, step):
        stacked = jnp.concatenate([w[at : at + step] for w in wide], axis=0)
        mixed = jnp.dot(row_perm, stacked, preferred_element_type=F32).astype(jnp.int32)
        out.append((mixed + base).astype(jnp.int8))
    return out


def _words(pieces):
    words = None
    for s, codes in enumerate(pieces):
        part = [w << s if s else w for w in _spread_rows(codes)]
        words = part if words is None else [a | b for a, b in zip(words, part)]
    return words


def _pack_rows_kernel(gate_ref, up_ref, lane_ref, row_ref, out_ref):
    rows = gate_ref.shape[1] // 4
    pieces = []
    for ref in (gate_ref, up_ref):
        codes = ref[...].T
        pieces += [codes[q * rows : (q + 1) * rows, :] for q in range(4)]
    at = 0
    for block in _interleave(_words(pieces), len(pieces), lane_ref[...], row_ref[...]):
        out_ref[at : at + block.shape[0], :] = block
        at += block.shape[0]


def _pack_cols_kernel(codes_ref, lane_ref, row_ref, *refs):
    out_ref = refs[-1]
    block = row_ref.shape[0] // 4
    lanes, rows = lane_ref[...], row_ref[...]

    def step(t, carry):
        codes = codes_ref[pl.ds(pl.multiple_of(t * block, block), block), :]
        pieces = [codes[:, q : q + 128] for q in range(0, codes.shape[1], 128)]
        (packed,) = _interleave(_words(pieces), len(pieces), lanes, rows)
        out_ref[pl.ds(pl.multiple_of(t * 4 * block, 4 * block), 4 * block), :] = packed
        return carry

    lax.fori_loop(0, codes_ref.shape[0] // block, step, 0)


def _lane_permutation():
    source = lax.broadcasted_iota(jnp.int32, (512, 512), 0)
    target = lax.broadcasted_iota(jnp.int32, (512, 512), 1)
    return (source == (target % 4) * 128 + target // 4).astype(BF16)


def _row_permutation(n):
    target = lax.broadcasted_iota(jnp.int32, (4 * n, 2 * n), 0)
    source = lax.broadcasted_iota(jnp.int32, (4 * n, 2 * n), 1)
    hit = source == (target % 2) * n + target // 4
    return jnp.where(hit, jnp.where(target % 4 < 2, 1, -1), 0).astype(BF16)


def pack_gate_up(gate_mask, up_mask):
    code_rows, code_cols = gate_mask.shape
    return pl.pallas_call(
        _pack_rows_kernel,
        grid=(pl.cdiv(code_cols, 128),),
        in_specs=[
            pl.BlockSpec((128, code_rows), lambda j: (j, 0)),
            pl.BlockSpec((128, code_rows), lambda j: (j, 0)),
            pl.BlockSpec((512, 512), lambda j: (0, 0)),
            pl.BlockSpec((128, 64), lambda j: (0, 0)),
        ],
        out_specs=pl.BlockSpec((code_rows, 512), lambda j: (0, j)),
        out_shape=jax.ShapeDtypeStruct((code_rows, 4 * code_cols), jnp.int8),
        compiler_params=pltpu.CompilerParams(vmem_limit_bytes=46 * 2**20),
        cost_estimate=COST,
        name="pack_gate_up",
    )(gate_mask.T, up_mask.T, _lane_permutation(), _row_permutation(32))


def pack_down(down_mask, after):
    return pl.pallas_call(
        _pack_cols_kernel,
        in_specs=[WHOLE] * 3 + [ANY] * len(after),
        out_specs=WHOLE,
        out_shape=jax.ShapeDtypeStruct((4 * down_mask.shape[0], 512), jnp.int8),
        compiler_params=pltpu.CompilerParams(vmem_limit_bytes=46 * 2**20),
        cost_estimate=COST,
        name="pack_down",
    )(down_mask, _lane_permutation(), _row_permutation(TILE // 4), *after)


def _bit(packed, s):
    if s == 7:
        return BF16(1) + (packed & jnp.int8(-128)).astype(BF16) * BF16(2.0**-7)
    return (packed & jnp.int8(1 << s)).astype(BF16) * BF16(2.0**-s)


def _rows_keep(packed, first):
    return jnp.concatenate([_bit(packed, first + q) for q in range(4)], axis=0)


def _cols_keep(packed, groups):
    return jnp.concatenate([_bit(packed, q) for q in range(groups)], axis=1)


def _tile(t):
    return pl.ds(pl.multiple_of(t * TILE, TILE), TILE)


class _Loads:
    def __init__(self, panels, bufs, sems, first, count):
        self.panels, self.bufs, self.sems, self.first, self.count = panels, bufs, sems, first, count

    def copy(self, k, t):
        panel, by_rows = self.panels[k]
        at = pl.ds(pl.multiple_of((self.first + t) * TILE, TILE), TILE)
        source = panel.at[at, :] if by_rows else panel.at[:, at]
        return pltpu.make_async_copy(source, self.bufs[k].at[t], self.sems.at[k, t])

    def start(self):
        for t in range(self.count):
            for k in range(len(self.panels)):
                self.copy(k, t).start()

    def copy_out(self, k, t):
        panel, by_rows = self.panels[k]
        at = pl.ds(pl.multiple_of((self.first + t) * TILE, TILE), TILE)
        target = panel.at[at, :] if by_rows else panel.at[:, at]
        return pltpu.make_async_copy(self.bufs[k].at[t], target, self.sems.at[k, t])

    def wait_out(self):
        for t in range(self.count):
            for k in range(len(self.panels)):
                self.copy_out(k, t).wait()

    def wait(self, t):
        for k in range(len(self.panels)):
            self.copy(k, t).wait()


def _load_scratch(panels, count):
    shapes = []
    for panel, by_rows in panels:
        block = (TILE, panel.shape[1]) if by_rows else (panel.shape[0], TILE)
        shapes.append(pltpu.VMEM((count, *block), panel.dtype))
    return shapes, pltpu.SemaphoreType.DMA((len(panels), count))


def _store_sums(at, t, sums, own_ref, to_x_ref, to_y_ref, mix_ref):
    half = sums.shape[0] // 8
    cut = lambda k, n=1: sums[k * half : (k + n) * half]
    lanes = _tile(t)
    own_ref[at, :, lanes] = cut(0, 2)
    to_x_ref[at, :half, lanes] = cut(2).astype(BF16)
    to_x_ref[at, half:, lanes] = cut(6).astype(BF16)
    to_y_ref[at, :half, lanes] = cut(5).astype(BF16)
    to_y_ref[at, half:, lanes] = cut(7).astype(BF16)
    mix_ref[at, :, lanes] = cut(3, 2)


def _gate_up_kernel(first, count, n_after, tok_ref, gate_any, up_any, bits_any, *refs):
    out_refs, (gate_buf, up_buf, bits_buf, sems) = refs[n_after : n_after + 4], refs[n_after + 4 :]
    loads = _Loads(
        [(gate_any, False), (up_any, False), (bits_any, False)], (gate_buf, up_buf, bits_buf), sems, first, count
    )
    loads.start()

    def step(t, carry):
        loads.wait(t)
        packed = bits_buf[t]
        for at, buf in enumerate((gate_buf, up_buf)):
            pruned = buf[t] * _rows_keep(packed, 4 * at)
            _store_sums(at, t, jnp.dot(tok_ref[...], pruned, preferred_element_type=F32), *out_refs)
        return carry

    lax.fori_loop(0, count, step, 0)


def _back_kernel(first, count, n_after, grad_ref, down_any, bits_any, *refs):
    out_refs, (down_buf, bits_buf, sems) = refs[n_after : n_after + 4], refs[n_after + 4 :]
    loads = _Loads([(down_any, True), (bits_any, True)], (down_buf, bits_buf), sems, first, count)
    loads.start()
    groups = grad_ref.shape[1] // 512

    def step(t, carry):
        loads.wait(t)
        pruned = down_buf[t] * _cols_keep(bits_buf[t], groups)
        _store_sums(0, t, contract_last(grad_ref[...], pruned), *out_refs)
        return carry

    lax.fori_loop(0, count, step, 0)


def _sum_shapes(n, rows, width):
    shape = lambda t: jax.ShapeDtypeStruct((n, rows // 4, width), t)
    return [shape(F32), shape(BF16), shape(BF16), shape(F32)]


def gate_up_sums(tok, gate_weight, up_weight, gate_up_bits, first, count, after=()):
    rows, depth = tok.shape
    bufs, sems = _load_scratch([(gate_weight, False), (up_weight, False), (gate_up_bits, False)], count)
    return pl.pallas_call(
        functools.partial(_gate_up_kernel, first, count, len(after)),
        in_specs=[WHOLE, HBM, HBM, HBM] + [ANY] * len(after),
        out_specs=[WHOLE] * 4,
        out_shape=_sum_shapes(2, rows, count * TILE),
        scratch_shapes=[*bufs, sems],
        compiler_params=pltpu.CompilerParams(vmem_limit_bytes=46 * 2**20),
        cost_estimate=COST,
        name="gate_up_sums",
    )(tok, gate_weight, up_weight, gate_up_bits, *after)


def back_sums(grads, down_weight, down_bits, first, count, after=()):
    rows, depth = grads.shape
    bufs, sems = _load_scratch([(down_weight, True), (down_bits, True)], count)
    return pl.pallas_call(
        functools.partial(_back_kernel, first, count, len(after)),
        in_specs=[WHOLE, HBM, HBM] + [ANY] * len(after),
        out_specs=[WHOLE] * 4,
        out_shape=_sum_shapes(1, rows, count * TILE),
        scratch_shapes=[*bufs, sems],
        compiler_params=pltpu.CompilerParams(vmem_limit_bytes=46 * 2**20),
        cost_estimate=COST,
        name="back_sums",
    )(grads, down_weight, down_bits, *after)


def _swap(value, bit):
    return lax.ppermute(value, "row", [(i, i ^ bit) for i in range(4)])


def _widen(parts):
    return jnp.concatenate(parts, axis=2) if len(parts) > 1 else parts[0]


class Reduction:
    def __init__(self):
        self.sums, self.received = [], []

    def first(self, sums):
        _, to_x, to_y, _ = sums
        self.sums.append(sums)
        self.received.append((_swap(to_x, 1), _swap(to_y, 2)))

    def mixed(self):
        half = self.sums[0][0].shape[1] // 2
        pairs = list(zip(self.sums, self.received))
        self.mixed_x = _widen([(s[3][:, :half] + r[1][:, half:]).astype(BF16) for s, r in pairs])
        self.mixed_y = _widen([(s[3][:, half:] + r[0][:, half:]).astype(BF16) for s, r in pairs])

    def second(self):
        self.second_x, self.second_y = _swap(self.mixed_x, 1), _swap(self.mixed_y, 2)

    def hold_first(self, until):
        self.received[-1] = _hold(self.received[-1], until)

    def hold_second(self, until):
        self.second_x, self.second_y = _hold((self.second_x, self.second_y), until)

    def total(self):
        half = self.sums[0][0].shape[1] // 2
        pairs = list(zip(self.sums, self.received))
        first_half = _widen([s[0][:, :half] + r[0][:, :half] for s, r in pairs]) + self.second_y
        second_half = _widen([s[0][:, half:] + r[1][:, :half] for s, r in pairs]) + self.second_x
        return jnp.concatenate([first_half, second_half], axis=1)


def _hold(values, until):
    return lax.optimization_barrier((values, until))[0]


class Gathering:
    def __init__(self, block):
        self.block = block

    def first(self):
        self.from_x, self.from_y = _swap(self.block, 1), _swap(self.block, 2)

    def hold_first(self, until):
        self.from_x, self.from_y = _hold((self.from_x, self.from_y), until)

    def cut(self):
        half = self.block.shape[1] // 2
        self.cut_x, self.cut_y = self.from_x[:, :half], self.from_y[:, half:]

    def second(self):
        diag_a, diag_b = _swap(self.cut_x, 2), _swap(self.cut_y, 1)
        self.blocks = (self.block, self.from_x, self.from_y, diag_a, diag_b)


def swiglu(gate_sum, up_sum):
    return (gate_sum * jax.nn.sigmoid(gate_sum) * up_sum).astype(BF16)


def swiglu_back(gate_sum, up_sum, back_sum):
    logistic = jax.nn.sigmoid(gate_sum)
    up_grad = back_sum * (gate_sum * logistic)
    gate_grad = back_sum * up_sum * logistic * (1.0 + gate_sum * (1.0 - logistic))
    return jnp.stack([gate_grad, up_grad]).astype(BF16)


def _backward_kernel(first, count, with_acc, with_input, with_weights, n_alias, n_after, *refs):
    refs = list(refs)
    take = lambda n: [refs.pop(0) for _ in range(n)]
    block_refs = take(5)
    panels = [(ref, False) for ref in take(1)]
    if with_input:
        panels += [(ref, False) for ref in take(2)]
        acc_refs = take(2) if with_acc else []
    if with_weights:
        (tok_ref,) = take(1)
        take(n_alias)
    take(n_after)
    sum_refs = take(2) if with_input else []
    outs = take(2) if with_weights else []
    bufs = take(len(panels))
    out_bufs = take(2) if with_weights else []
    load_sems = refs.pop(0)
    loads = _Loads(panels, bufs, load_sems, first, count)
    stores = _Loads([(ref, False) for ref in outs], out_bufs, refs.pop(0), first, count) if with_weights else None
    loads.start()
    if with_input:
        for k, ref in enumerate(sum_refs):
            ref[...] = acc_refs[k][...] if with_acc else jnp.zeros_like(ref)

    def step(t, carry):
        loads.wait(t)
        lanes = _tile(t)
        rows_of = lambda k: jnp.concatenate([ref[k, :, lanes] for ref in block_refs], axis=0)
        packed = bufs[0][t]
        gate_keep, up_keep = _rows_keep(packed, 0), _rows_keep(packed, 4)
        gate_grad, up_grad = rows_of(0), rows_of(1)
        if with_weights:
            tok = tok_ref[...]
            out_bufs[0][t] = contract_first(tok, gate_grad).astype(BF16) * gate_keep
            stores.copy_out(0, t).start()
            out_bufs[1][t] = contract_first(tok, up_grad).astype(BF16) * up_keep
            stores.copy_out(1, t).start()
        if with_input:
            part = contract_last(gate_grad, bufs[1][t] * gate_keep) + contract_last(up_grad, bufs[2][t] * up_keep)
            half = sum_refs[0].shape[1]
            for p in range(4):
                for k, ref in enumerate(sum_refs):
                    ref[p] += part[(2 * p + k) * half : (2 * p + k + 1) * half]
        return carry

    lax.fori_loop(0, count, step, 0)
    if with_weights:
        stores.wait_out()


def backward(blocks, gate_up_bits, first, count, inputs=None, weights=None, after=()):
    args, specs, shapes, out_specs, aliases = list(blocks), [WHOLE] * 5, [], [], {}
    rows = 4 * blocks[0].shape[1]
    depth = 4 * gate_up_bits.shape[0]
    width = gate_up_bits.shape[1]
    panels, outs = [(gate_up_bits, False)], []
    args.append(gate_up_bits)
    specs.append(HBM)
    if inputs is not None:
        gate_weight, up_weight, acc = inputs
        panels += [(gate_weight, False), (up_weight, False)]
        args += [gate_weight, up_weight]
        specs += [HBM, HBM]
        if acc is not None:
            args += acc
            specs += [WHOLE] * 2
        shapes += [jax.ShapeDtypeStruct((4, rows // 8, depth), F32)] * 2
        out_specs += [WHOLE] * 2
    n_alias = 0
    if weights is not None:
        tok, so_far = weights
        args.append(tok)
        specs.append(WHOLE)
        if so_far is not None:
            n_alias = 2
            for k, value in enumerate(so_far):
                aliases[len(args)] = len(shapes) + k
                args.append(value)
                specs.append(HBM)
        outs = [jax.ShapeDtypeStruct((depth, width), BF16)] * 2
        shapes += outs
        out_specs += [HBM] * 2
    bufs, sems = _load_scratch(panels, count)
    scratch = [*bufs, sems]
    if weights is not None:
        out_bufs, out_sems = _load_scratch([(out, False) for out in outs], count)
        scratch = [*bufs, *out_bufs, sems, out_sems]
    args += list(after)
    specs += [ANY] * len(after)
    return pl.pallas_call(
        functools.partial(
            _backward_kernel,
            first,
            count,
            inputs is not None and inputs[2] is not None,
            inputs is not None,
            weights is not None,
            n_alias,
            len(after),
        ),
        in_specs=specs,
        out_specs=out_specs,
        out_shape=shapes,
        scratch_shapes=scratch,
        input_output_aliases=aliases,
        compiler_params=pltpu.CompilerParams(vmem_limit_bytes=46 * 2**20),
        cost_estimate=COST,
        name="backward",
    )(*args)


def _down_grad_kernel(count, n_after, *refs):
    block_refs, (grad_ref, bits_any), (out_any, bits_buf, out_buf, sems, out_sems) = refs[:5], refs[5:7], refs[7 + n_after :]
    loads = _Loads([(bits_any, True)], [bits_buf], sems, 0, count)
    stores = _Loads([(out_any, True)], [out_buf], out_sems, 0, count)
    loads.start()

    def step(t, carry):
        loads.wait(t)
        hidden = jnp.concatenate([ref[0, :, _tile(t)] for ref in block_refs], axis=0)
        keep = _cols_keep(bits_buf[t], grad_ref.shape[1] // 512)
        out_buf[t] = contract_first(hidden, grad_ref[...]).astype(BF16) * keep
        stores.copy_out(0, t).start()
        return carry

    lax.fori_loop(0, count, step, 0)
    stores.wait_out()


def down_grad(blocks, grads, down_bits, after=()):
    width, depth = down_bits.shape[0], grads.shape[1]
    count = width // TILE
    out = jax.ShapeDtypeStruct((width, depth), BF16)
    (bits_buf,), sems = _load_scratch([(down_bits, True)], count)
    (out_buf,), out_sems = _load_scratch([(out, True)], count)
    return pl.pallas_call(
        functools.partial(_down_grad_kernel, count, len(after)),
        in_specs=[WHOLE] * 6 + [HBM] + [ANY] * len(after),
        out_specs=HBM,
        out_shape=out,
        scratch_shapes=[bits_buf, out_buf, sems, out_sems],
        compiler_params=pltpu.CompilerParams(vmem_limit_bytes=46 * 2**20),
        cost_estimate=COST,
        name="down_grad",
    )(*blocks, grads, down_bits, *after)


def _col_swap(value, bits):
    return lax.ppermute(value, "col", [(i, i ^ bits) for i in range(8)])


def gather_groups(value):
    return [value] + [_col_swap(value, 2 * k) for k in (1, 2, 3)]


def order_groups(mine, theirs, order):
    groups = []
    for p in range(4):
        for part in (mine, theirs):
            groups.append(lax.dynamic_index_in_dim(part, p ^ order, 0, keepdims=False))
    return jnp.concatenate(groups, axis=0)


def chunks_of(tiles, cuts):
    ends = [0] + [(tiles * c + 6) // 13 for c in cuts]
    return [(a, b - a) for a, b in zip(ends[:-1], ends[1:])]


def local_tiled(tokens, out_grad, gate_weight, up_weight, down_weight, gate_mask, up_mask, down_mask):
    order = lax.axis_index("row") ^ (lax.axis_index("col") // 2)
    tiles = gate_weight.shape[1] // TILE
    gate_up_bits = pack_gate_up(gate_mask, up_mask)
    tok_mine, gate_up_bits = lax.optimization_barrier((gather_groups(tokens), gate_up_bits))
    tok_mine = jnp.stack(tok_mine)
    tok_theirs = _col_swap(tok_mine, 1)
    tok = order_groups(tok_mine, tok_theirs, order)
    gate_up = lambda c, after: gate_up_sums(tok, gate_weight, up_weight, gate_up_bits, *c, after=after)
    back = lambda c, after: back_sums(grads, down_weight, down_bits, *c, after=after)
    gate_up_red, back_red = Reduction(), [Reduction(), Reduction()]

    cuts = chunks_of(tiles, GATE_UP_CUTS)
    sums0 = gate_up(cuts[0], [])
    gate_up_red.first(sums0)
    sums1 = gate_up(cuts[1], [sums0[0]])
    gate_up_red.hold_first(sums1[0])
    gate_up_red.first(sums1)
    grad_mine = gather_groups(_hold(out_grad, sums1[0]))
    down_bits = pack_down(down_mask, [sums1[0], *gate_up_red.received[0]])
    gate_up_red.hold_first(down_bits)
    grad_mine = jnp.stack(_hold(grad_mine, down_bits))
    grad_theirs = _col_swap(grad_mine, 1)
    gate_up_red.mixed()
    gate_up_red.second()
    grads = order_groups(grad_mine, grad_theirs, order)
    cuts = chunks_of(tiles, BACK_CUTS)
    sums0 = back(cuts[0], [gate_up_red.mixed_x, gate_up_red.mixed_y])
    back_red[0].first(sums0)
    sums1 = back(cuts[1], [sums0[0]])
    back_red[0].hold_first(sums1[0])
    sums1 = _hold(sums1, back_red[0].received[0])
    gate_up_red.hold_second(sums1[0])
    back_red[0].mixed()
    back_red[0].second()
    back_red[1].first(sums1)
    gate_up_total = gate_up_red.total()
    hidden = Gathering(swiglu(*gate_up_total)[None])
    gate_up_total = _hold(gate_up_total, hidden.block)
    split = cuts[1][0] * TILE
    gath = [Gathering(swiglu_back(*gate_up_total[:, :, :split], *back_red[0].total()))]
    gath[0].first()
    back_red[1].hold_first(gath[0].block)
    back_red[1].mixed()
    back_red[1].second()
    gath[0].hold_first(back_red[1].mixed_x)
    gath[0].cut()
    gath[0].second()
    gath.append(Gathering(swiglu_back(*gate_up_total[:, :, split:], *back_red[1].total())))
    gath[1].first()
    pair = (gate_weight, up_weight)
    acc = backward(gath[0].blocks, gate_up_bits, *cuts[0], inputs=(*pair, None), after=[gath[1].block])
    gath[1].hold_first(acc[0])
    gath[1].cut()
    gath[1].second()
    hidden.block = _hold(hidden.block, gath[1].blocks[3:])
    hidden.first()
    outs = backward(gath[0].blocks, gate_up_bits, *cuts[0], weights=(tok, None), after=[gath[1].cut_x, gath[1].cut_y])
    acc = backward(gath[1].blocks, gate_up_bits, *cuts[1], inputs=(*pair, acc), after=[outs[0]])
    hidden.hold_first(acc[0])
    hidden.cut()
    acc = _hold(acc, (hidden.cut_x, hidden.cut_y))
    hidden.second()
    pairs = acc[0] + _col_swap(acc[1], 1)
    own = lax.dynamic_index_in_dim(pairs, order, 0, keepdims=False)
    sent = [lax.dynamic_index_in_dim(pairs, k ^ order, 0, keepdims=False).astype(BF16) for k in (1, 2, 3)]
    received = [_col_swap(value, 2 * k) for k, value in zip((1, 2, 3), sent)]
    outs = backward(gath[1].blocks, gate_up_bits, *cuts[1], weights=(tok, outs), after=sent)
    down_out = down_grad(hidden.blocks, grads, down_bits, [outs[0]])
    for value in received:
        own = own + value
    return (own.astype(BF16), *outs, down_out)


def tiled_fits(mesh, depth, width, token_rows):
    return (
        mesh.shape["row"] == 4
        and mesh.shape["col"] == 8
        and depth % 1280 == 0
        and depth // 512 <= 7
        and depth % 512 == 0
        and width % TILE == 0
        and width // TILE >= 13
        and token_rows % 256 == 0
    )


def solution(mesh):
    in_specs = (
        P("col", "row"),
        P("col", "row"),
        P("row", "col"),
        P("row", "col"),
        P("col", "row"),
        P("row", "col"),
        P("row", "col"),
        P("col", "row"),
    )
    out_specs = (P("col", "row"), P("row", "col"), P("row", "col"), P("col", "row"))

    def run(tokens, out_grad, gate_weight, *rest):
        depth = gate_weight.shape[0] // mesh.shape["row"]
        width = gate_weight.shape[1] // mesh.shape["col"]
        body = local_tiled if tiled_fits(mesh, depth, width, tokens.shape[0]) else local_any
        mapped = jax.shard_map(body, mesh=mesh, in_specs=in_specs, out_specs=out_specs, check_vma=False)
        return mapped(tokens, out_grad, gate_weight, *rest)

    return run
```

```python
import functools

import jax
import jax.numpy as jnp
from jax import lax
from jax.experimental import pallas as pl
from jax.experimental.pallas import tpu as pltpu
from jax.sharding import PartitionSpec as P

BF16 = jnp.bfloat16
F32 = jnp.float32
COST = pl.CostEstimate(flops=10**10, bytes_accessed=10**8, transcendentals=0)
TILE = 256
ANY = pl.BlockSpec(memory_space=pl.ANY)
HBM = pl.BlockSpec(memory_space=pltpu.HBM)
WHOLE = pl.BlockSpec(memory_space=pltpu.VMEM)
GATE_UP_CUTS = (7, 13)
BACK_CUTS = (4, 13)


def expand_mask(block_ids):
    lead_col = block_ids // 6
    second_rank = block_ids // 2 % 3
    third_rank = block_ids % 2
    second_col = second_rank + (second_rank >= lead_col).astype(jnp.int32)
    low_col = jnp.minimum(lead_col, second_col)
    high_col = jnp.maximum(lead_col, second_col)
    rest_low = jnp.where(low_col > 0, 0, jnp.where(high_col > 1, 1, 2)).astype(jnp.int32)
    rest_high = 6 - low_col - high_col - rest_low
    third_col = jnp.where(third_rank == 0, rest_low, rest_high)
    fourth_col = 6 - lead_col - second_col - third_col
    ordering = [lead_col, second_col, third_col, fourth_col]
    group_rows, group_cols = block_ids.shape
    col_position = lax.broadcasted_iota(jnp.int32, (group_rows, 4 * group_cols), 1) % 4
    row_list = []
    for local_row in range(4):
        current = jnp.repeat(ordering[local_row], 4, axis=1)
        following = jnp.repeat(ordering[(local_row + 1) % 4], 4, axis=1)
        row_list.append((current == col_position) | (following == col_position))
    pattern = jnp.stack(row_list, axis=1).reshape(4 * group_rows, 4 * group_cols)
    return pattern.astype(jnp.bfloat16)


def contract_last(left, right):
    return lax.dot_general(
        left, right, (((1,), (1,)), ((), ())), preferred_element_type=jnp.float32
    )


def contract_first(left, right):
    return lax.dot_general(
        left, right, (((0,), (0,)), ((), ())), preferred_element_type=jnp.float32
    )


def local_any(tokens, out_grad, gate_weight, up_weight, down_weight, gate_mask, up_mask, down_mask):
    gate_keep = expand_mask(gate_mask)
    up_keep = expand_mask(up_mask)
    down_keep = expand_mask(down_mask)
    gate_pruned = gate_weight * gate_keep
    up_pruned = up_weight * up_keep
    down_pruned = down_weight * down_keep
    panel_width = gate_pruned.shape[1]
    all_tokens, all_grads = (
        lax.all_gather(tokens, "col", axis=0, tiled=True),
        lax.all_gather(out_grad, "col", axis=0, tiled=True),
    )
    gate_sum = jnp.dot(all_tokens, gate_pruned, preferred_element_type=jnp.float32)
    up_sum = jnp.dot(all_tokens, up_pruned, preferred_element_type=jnp.float32)
    back_sum = contract_last(all_grads, down_pruned)
    shares = lax.psum_scatter(
        jnp.concatenate([gate_sum, up_sum, back_sum], axis=1),
        "row",
        scatter_dimension=0,
        tiled=True,
    )
    gate_sum = shares[:, :panel_width]
    up_sum = shares[:, panel_width : 2 * panel_width]
    back_sum = shares[:, 2 * panel_width :]
    logistic = jax.nn.sigmoid(gate_sum)
    swish_val = gate_sum * logistic
    hidden = swish_val * up_sum
    swiglu_up_grad = back_sum * swish_val
    swiglu_gate_grad = back_sum * up_sum * logistic * (1.0 + gate_sum * (1.0 - logistic))
    local_grads = jnp.concatenate([swiglu_gate_grad, swiglu_up_grad, hidden], axis=1).astype(
        jnp.bfloat16
    )
    all_local = lax.all_gather(local_grads, "row", axis=0, tiled=True)
    gate_grad = all_local[:, :panel_width]
    up_grad = all_local[:, panel_width : 2 * panel_width]
    hidden = all_local[:, 2 * panel_width :]
    input_grad = lax.psum_scatter(
        contract_last(gate_grad, gate_pruned) + contract_last(up_grad, up_pruned),
        "col",
        scatter_dimension=0,
        tiled=True,
    ).astype(jnp.bfloat16)
    gate_weight_grad = (contract_first(all_tokens, gate_grad) * gate_keep).astype(jnp.bfloat16)
    up_weight_grad = (contract_first(all_tokens, up_grad) * up_keep).astype(jnp.bfloat16)
    down_weight_grad = (contract_first(hidden, all_grads) * down_keep).astype(jnp.bfloat16)
    return (input_grad, gate_weight_grad, up_weight_grad, down_weight_grad)


def _spread_rows(codes):
    byte = lambda k: jnp.int32(1 << (8 * k))
    is0, is01, is012 = codes < 6, codes < 12, codes < 18
    first = jnp.where(is0, byte(0), jnp.where(is01, byte(1), jnp.where(is012, byte(2), byte(3))))
    rest = codes - jnp.where(is0, 0, jnp.where(is01, 6, jnp.where(is012, 12, 18)))
    low = jnp.where(is0, byte(1), byte(0))
    mid = jnp.where(is01, byte(2), byte(1))
    high = jnp.where(is012, byte(3), byte(2))
    early, late = rest < 2, rest < 4
    second = jnp.where(early, low, jnp.where(late, mid, high))
    third = jnp.where((rest & 1) == 0, jnp.where(early, mid, low), jnp.where(late, high, mid))
    return first | second, second | third


def _interleave(words, count, lane_perm, row_perm):
    rows = words[0].shape[0]
    wide = []
    for w in words:
        planes = [(lax.shift_right_logical(w, jnp.int32(8 * j)) & 255).astype(F32).astype(BF16) for j in range(4)]
        wide.append(jnp.dot(jnp.concatenate(planes, axis=1), lane_perm, preferred_element_type=F32).astype(BF16))
    step = row_perm.shape[0] // 4
    local_row = lax.broadcasted_iota(jnp.int32, (4 * step, 512), 0) % 4
    bias = 128 if count == 8 else 0
    base = jnp.where(local_row < 2, -bias, (1 << count) - 1 - bias)
    out = []
    for at in range(0, rows, step):
        stacked = jnp.concatenate([w[at : at + step] for w in wide], axis=0)
        mixed = jnp.dot(row_perm, stacked, preferred_element_type=F32).astype(jnp.int32)
        out.append((mixed + base).astype(jnp.int8))
    return out


def _words(pieces):
    words = None
    for s, codes in enumerate(pieces):
        part = [w << s if s else w for w in _spread_rows(codes)]
        words = part if words is None else [a | b for a, b in zip(words, part)]
    return words


def _pack_rows_kernel(gate_ref, up_ref, lane_ref, row_ref, out_ref):
    rows = gate_ref.shape[1] // 4
    pieces = []
    for ref in (gate_ref, up_ref):
        codes = ref[...].T
        pieces += [codes[q * rows : (q + 1) * rows, :] for q in range(4)]
    at = 0
    for block in _interleave(_words(pieces), len(pieces), lane_ref[...], row_ref[...]):
        out_ref[at : at + block.shape[0], :] = block
        at += block.shape[0]


def _pack_cols_kernel(codes_ref, lane_ref, row_ref, *refs):
    out_ref = refs[-1]
    block = row_ref.shape[0] // 4
    lanes, rows = lane_ref[...], row_ref[...]

    def step(t, carry):
        codes = codes_ref[pl.ds(pl.multiple_of(t * block, block), block), :]
        pieces = [codes[:, q : q + 128] for q in range(0, codes.shape[1], 128)]
        (packed,) = _interleave(_words(pieces), len(pieces), lanes, rows)
        out_ref[pl.ds(pl.multiple_of(t * 4 * block, 4 * block), 4 * block), :] = packed
        return carry

    lax.fori_loop(0, codes_ref.shape[0] // block, step, 0)


def _lane_permutation():
    source = lax.broadcasted_iota(jnp.int32, (512, 512), 0)
    target = lax.broadcasted_iota(jnp.int32, (512, 512), 1)
    return (source == (target % 4) * 128 + target // 4).astype(BF16)


def _row_permutation(n):
    target = lax.broadcasted_iota(jnp.int32, (4 * n, 2 * n), 0)
    source = lax.broadcasted_iota(jnp.int32, (4 * n, 2 * n), 1)
    hit = source == (target % 2) * n + target // 4
    return jnp.where(hit, jnp.where(target % 4 < 2, 1, -1), 0).astype(BF16)


def pack_gate_up(gate_mask, up_mask):
    code_rows, code_cols = gate_mask.shape
    return pl.pallas_call(
        _pack_rows_kernel,
        grid=(pl.cdiv(code_cols, 128),),
        in_specs=[
            pl.BlockSpec((128, code_rows), lambda j: (j, 0)),
            pl.BlockSpec((128, code_rows), lambda j: (j, 0)),
            pl.BlockSpec((512, 512), lambda j: (0, 0)),
            pl.BlockSpec((128, 64), lambda j: (0, 0)),
        ],
        out_specs=pl.BlockSpec((code_rows, 512), lambda j: (0, j)),
        out_shape=jax.ShapeDtypeStruct((code_rows, 4 * code_cols), jnp.int8),
        compiler_params=pltpu.CompilerParams(vmem_limit_bytes=46 * 2**20),
        cost_estimate=COST,
        name="pack_gate_up",
    )(gate_mask.T, up_mask.T, _lane_permutation(), _row_permutation(32))


def pack_down(down_mask, after):
    return pl.pallas_call(
        _pack_cols_kernel,
        in_specs=[WHOLE] * 3 + [ANY] * len(after),
        out_specs=WHOLE,
        out_shape=jax.ShapeDtypeStruct((4 * down_mask.shape[0], 512), jnp.int8),
        compiler_params=pltpu.CompilerParams(vmem_limit_bytes=46 * 2**20),
        cost_estimate=COST,
        name="pack_down",
    )(down_mask, _lane_permutation(), _row_permutation(TILE // 4), *after)


def _bit(packed, s):
    if s == 7:
        return BF16(1) + (packed & jnp.int8(-128)).astype(BF16) * BF16(2.0**-7)
    return (packed & jnp.int8(1 << s)).astype(BF16) * BF16(2.0**-s)


def _rows_keep(packed, first):
    return jnp.concatenate([_bit(packed, first + q) for q in range(4)], axis=0)


def _cols_keep(packed, groups):
    return jnp.concatenate([_bit(packed, q) for q in range(groups)], axis=1)


def _tile(t):
    return pl.ds(pl.multiple_of(t * TILE, TILE), TILE)


class _Loads:
    def __init__(self, panels, bufs, sems, first, count):
        self.panels, self.bufs, self.sems, self.first, self.count = panels, bufs, sems, first, count

    def copy(self, k, t):
        panel, by_rows = self.panels[k]
        at = pl.ds(pl.multiple_of((self.first + t) * TILE, TILE), TILE)
        source = panel.at[at, :] if by_rows else panel.at[:, at]
        return pltpu.make_async_copy(source, self.bufs[k].at[t], self.sems.at[k, t])

    def start(self):
        for t in range(self.count):
            for k in range(len(self.panels)):
                self.copy(k, t).start()

    def copy_out(self, k, t):
        panel, by_rows = self.panels[k]
        at = pl.ds(pl.multiple_of((self.first + t) * TILE, TILE), TILE)
        target = panel.at[at, :] if by_rows else panel.at[:, at]
        return pltpu.make_async_copy(self.bufs[k].at[t], target, self.sems.at[k, t])

    def wait_out(self):
        for t in range(self.count):
            for k in range(len(self.panels)):
                self.copy_out(k, t).wait()

    def wait(self, t):
        for k in range(len(self.panels)):
            self.copy(k, t).wait()


def _load_scratch(panels, count):
    shapes = []
    for panel, by_rows in panels:
        block = (TILE, panel.shape[1]) if by_rows else (panel.shape[0], TILE)
        shapes.append(pltpu.VMEM((count, *block), panel.dtype))
    return shapes, pltpu.SemaphoreType.DMA((len(panels), count))


def _store_sums(at, t, sums, own_ref, to_x_ref, to_y_ref, mix_ref):
    half = sums.shape[0] // 8
    cut = lambda k, n=1: sums[k * half : (k + n) * half]
    lanes = _tile(t)
    own_ref[at, :, lanes] = cut(0, 2)
    to_x_ref[at, :half, lanes] = cut(2).astype(BF16)
    to_x_ref[at, half:, lanes] = cut(6).astype(BF16)
    to_y_ref[at, :half, lanes] = cut(5).astype(BF16)
    to_y_ref[at, half:, lanes] = cut(7).astype(BF16)
    mix_ref[at, :, lanes] = cut(3, 2)


def _gate_up_kernel(first, count, n_after, tok_ref, gate_any, up_any, bits_any, *refs):
    out_refs, (gate_buf, up_buf, bits_buf, sems) = refs[n_after : n_after + 4], refs[n_after + 4 :]
    loads = _Loads(
        [(gate_any, False), (up_any, False), (bits_any, False)], (gate_buf, up_buf, bits_buf), sems, first, count
    )
    loads.start()

    def step(t, carry):
        loads.wait(t)
        packed = bits_buf[t]
        for at, buf in enumerate((gate_buf, up_buf)):
            pruned = buf[t] * _rows_keep(packed, 4 * at)
            _store_sums(at, t, jnp.dot(tok_ref[...], pruned, preferred_element_type=F32), *out_refs)
        return carry

    lax.fori_loop(0, count, step, 0)


def _back_kernel(first, count, n_after, grad_ref, down_any, bits_any, *refs):
    out_refs, (down_buf, bits_buf, sems) = refs[n_after : n_after + 4], refs[n_after + 4 :]
    loads = _Loads([(down_any, True), (bits_any, True)], (down_buf, bits_buf), sems, first, count)
    loads.start()
    groups = grad_ref.shape[1] // 512

    def step(t, carry):
        loads.wait(t)
        pruned = down_buf[t] * _cols_keep(bits_buf[t], groups)
        _store_sums(0, t, contract_last(grad_ref[...], pruned), *out_refs)
        return carry

    lax.fori_loop(0, count, step, 0)


def _sum_shapes(n, rows, width):
    shape = lambda t: jax.ShapeDtypeStruct((n, rows // 4, width), t)
    return [shape(F32), shape(BF16), shape(BF16), shape(F32)]


def gate_up_sums(tok, gate_weight, up_weight, gate_up_bits, first, count, after=()):
    rows, depth = tok.shape
    bufs, sems = _load_scratch([(gate_weight, False), (up_weight, False), (gate_up_bits, False)], count)
    return pl.pallas_call(
        functools.partial(_gate_up_kernel, first, count, len(after)),
        in_specs=[WHOLE, HBM, HBM, HBM] + [ANY] * len(after),
        out_specs=[WHOLE] * 4,
        out_shape=_sum_shapes(2, rows, count * TILE),
        scratch_shapes=[*bufs, sems],
        compiler_params=pltpu.CompilerParams(vmem_limit_bytes=46 * 2**20),
        cost_estimate=COST,
        name="gate_up_sums",
    )(tok, gate_weight, up_weight, gate_up_bits, *after)


def back_sums(grads, down_weight, down_bits, first, count, after=()):
    rows, depth = grads.shape
    bufs, sems = _load_scratch([(down_weight, True), (down_bits, True)], count)
    return pl.pallas_call(
        functools.partial(_back_kernel, first, count, len(after)),
        in_specs=[WHOLE, HBM, HBM] + [ANY] * len(after),
        out_specs=[WHOLE] * 4,
        out_shape=_sum_shapes(1, rows, count * TILE),
        scratch_shapes=[*bufs, sems],
        compiler_params=pltpu.CompilerParams(vmem_limit_bytes=46 * 2**20),
        cost_estimate=COST,
        name="back_sums",
    )(grads, down_weight, down_bits, *after)


def _swap(value, bit):
    return lax.ppermute(value, "row", [(i, i ^ bit) for i in range(4)])


def _widen(parts):
    return jnp.concatenate(parts, axis=2) if len(parts) > 1 else parts[0]


class Reduction:
    def __init__(self):
        self.sums, self.received = [], []

    def first(self, sums):
        _, to_x, to_y, _ = sums
        self.sums.append(sums)
        self.received.append((_swap(to_x, 1), _swap(to_y, 2)))

    def mixed(self):
        half = self.sums[0][0].shape[1] // 2
        pairs = list(zip(self.sums, self.received))
        self.mixed_x = _widen([(s[3][:, :half] + r[1][:, half:]).astype(BF16) for s, r in pairs])
        self.mixed_y = _widen([(s[3][:, half:] + r[0][:, half:]).astype(BF16) for s, r in pairs])

    def second(self):
        self.second_x, self.second_y = _swap(self.mixed_x, 1), _swap(self.mixed_y, 2)

    def hold_first(self, until):
        self.received[-1] = _hold(self.received[-1], until)

    def hold_second(self, until):
        self.second_x, self.second_y = _hold((self.second_x, self.second_y), until)

    def total(self):
        half = self.sums[0][0].shape[1] // 2
        pairs = list(zip(self.sums, self.received))
        first_half = _widen([s[0][:, :half] + r[0][:, :half] for s, r in pairs]) + self.second_y
        second_half = _widen([s[0][:, half:] + r[1][:, :half] for s, r in pairs]) + self.second_x
        return jnp.concatenate([first_half, second_half], axis=1)


def _hold(values, until):
    return lax.optimization_barrier((values, until))[0]


class Gathering:
    def __init__(self, block):
        self.block = block

    def first(self):
        self.from_x, self.from_y = _swap(self.block, 1), _swap(self.block, 2)

    def hold_first(self, until):
        self.from_x, self.from_y = _hold((self.from_x, self.from_y), until)

    def cut(self):
        half = self.block.shape[1] // 2
        self.cut_x, self.cut_y = self.from_x[:, :half], self.from_y[:, half:]

    def second(self):
        diag_a, diag_b = _swap(self.cut_x, 2), _swap(self.cut_y, 1)
        self.blocks = (self.block, self.from_x, self.from_y, diag_a, diag_b)


def swiglu(gate_sum, up_sum):
    return (gate_sum * jax.nn.sigmoid(gate_sum) * up_sum).astype(BF16)


def swiglu_back(gate_sum, up_sum, back_sum):
    logistic = jax.nn.sigmoid(gate_sum)
    up_grad = back_sum * (gate_sum * logistic)
    gate_grad = back_sum * up_sum * logistic * (1.0 + gate_sum * (1.0 - logistic))
    return jnp.stack([gate_grad, up_grad]).astype(BF16)


def _backward_kernel(first, count, with_acc, with_input, with_weights, n_alias, n_after, *refs):
    refs = list(refs)
    take = lambda n: [refs.pop(0) for _ in range(n)]
    block_refs = take(5)
    panels = [(ref, False) for ref in take(1)]
    if with_input:
        panels += [(ref, False) for ref in take(2)]
        acc_refs = take(2) if with_acc else []
    if with_weights:
        (tok_ref,) = take(1)
        take(n_alias)
    take(n_after)
    sum_refs = take(2) if with_input else []
    outs = take(2) if with_weights else []
    bufs = take(len(panels))
    out_bufs = take(2) if with_weights else []
    load_sems = refs.pop(0)
    loads = _Loads(panels, bufs, load_sems, first, count)
    stores = _Loads([(ref, False) for ref in outs], out_bufs, refs.pop(0), first, count) if with_weights else None
    loads.start()
    if with_input:
        for k, ref in enumerate(sum_refs):
            ref[...] = acc_refs[k][...] if with_acc else jnp.zeros_like(ref)

    def step(t, carry):
        loads.wait(t)
        lanes = _tile(t)
        rows_of = lambda k: jnp.concatenate([ref[k, :, lanes] for ref in block_refs], axis=0)
        packed = bufs[0][t]
        gate_keep, up_keep = _rows_keep(packed, 0), _rows_keep(packed, 4)
        gate_grad, up_grad = rows_of(0), rows_of(1)
        if with_weights:
            tok = tok_ref[...]
            out_bufs[0][t] = contract_first(tok, gate_grad).astype(BF16) * gate_keep
            stores.copy_out(0, t).start()
            out_bufs[1][t] = contract_first(tok, up_grad).astype(BF16) * up_keep
            stores.copy_out(1, t).start()
        if with_input:
            part = contract_last(gate_grad, bufs[1][t] * gate_keep) + contract_last(up_grad, bufs[2][t] * up_keep)
            half = sum_refs[0].shape[1]
            for p in range(4):
                for k, ref in enumerate(sum_refs):
                    ref[p] += part[(2 * p + k) * half : (2 * p + k + 1) * half]
        return carry

    lax.fori_loop(0, count, step, 0)
    if with_weights:
        stores.wait_out()


def backward(blocks, gate_up_bits, first, count, inputs=None, weights=None, after=()):
    args, specs, shapes, out_specs, aliases = list(blocks), [WHOLE] * 5, [], [], {}
    rows = 4 * blocks[0].shape[1]
    depth = 4 * gate_up_bits.shape[0]
    width = gate_up_bits.shape[1]
    panels, outs = [(gate_up_bits, False)], []
    args.append(gate_up_bits)
    specs.append(HBM)
    if inputs is not None:
        gate_weight, up_weight, acc = inputs
        panels += [(gate_weight, False), (up_weight, False)]
        args += [gate_weight, up_weight]
        specs += [HBM, HBM]
        if acc is not None:
            args += acc
            specs += [WHOLE] * 2
        shapes += [jax.ShapeDtypeStruct((4, rows // 8, depth), F32)] * 2
        out_specs += [WHOLE] * 2
    n_alias = 0
    if weights is not None:
        tok, so_far = weights
        args.append(tok)
        specs.append(WHOLE)
        if so_far is not None:
            n_alias = 2
            for k, value in enumerate(so_far):
                aliases[len(args)] = len(shapes) + k
                args.append(value)
                specs.append(HBM)
        outs = [jax.ShapeDtypeStruct((depth, width), BF16)] * 2
        shapes += outs
        out_specs += [HBM] * 2
    bufs, sems = _load_scratch(panels, count)
    scratch = [*bufs, sems]
    if weights is not None:
        out_bufs, out_sems = _load_scratch([(out, False) for out in outs], count)
        scratch = [*bufs, *out_bufs, sems, out_sems]
    args += list(after)
    specs += [ANY] * len(after)
    return pl.pallas_call(
        functools.partial(
            _backward_kernel,
            first,
            count,
            inputs is not None and inputs[2] is not None,
            inputs is not None,
            weights is not None,
            n_alias,
            len(after),
        ),
        in_specs=specs,
        out_specs=out_specs,
        out_shape=shapes,
        scratch_shapes=scratch,
        input_output_aliases=aliases,
        compiler_params=pltpu.CompilerParams(vmem_limit_bytes=46 * 2**20),
        cost_estimate=COST,
        name="backward",
    )(*args)


def _down_grad_kernel(count, n_after, *refs):
    block_refs, (grad_ref, bits_any), (out_any, bits_buf, out_buf, sems, out_sems) = refs[:5], refs[5:7], refs[7 + n_after :]
    loads = _Loads([(bits_any, True)], [bits_buf], sems, 0, count)
    stores = _Loads([(out_any, True)], [out_buf], out_sems, 0, count)
    loads.start()

    def step(t, carry):
        loads.wait(t)
        hidden = jnp.concatenate([ref[0, :, _tile(t)] for ref in block_refs], axis=0)
        keep = _cols_keep(bits_buf[t], grad_ref.shape[1] // 512)
        out_buf[t] = contract_first(hidden, grad_ref[...]).astype(BF16) * keep
        stores.copy_out(0, t).start()
        return carry

    lax.fori_loop(0, count, step, 0)
    stores.wait_out()


def down_grad(blocks, grads, down_bits, after=()):
    width, depth = down_bits.shape[0], grads.shape[1]
    count = width // TILE
    out = jax.ShapeDtypeStruct((width, depth), BF16)
    (bits_buf,), sems = _load_scratch([(down_bits, True)], count)
    (out_buf,), out_sems = _load_scratch([(out, True)], count)
    return pl.pallas_call(
        functools.partial(_down_grad_kernel, count, len(after)),
        in_specs=[WHOLE] * 6 + [HBM] + [ANY] * len(after),
        out_specs=HBM,
        out_shape=out,
        scratch_shapes=[bits_buf, out_buf, sems, out_sems],
        compiler_params=pltpu.CompilerParams(vmem_limit_bytes=46 * 2**20),
        cost_estimate=COST,
        name="down_grad",
    )(*blocks, grads, down_bits, *after)


def _col_swap(value, bits):
    return lax.ppermute(value, "col", [(i, i ^ bits) for i in range(8)])


def gather_groups(value):
    return [value] + [_col_swap(value, 2 * k) for k in (1, 2, 3)]


def order_groups(mine, theirs, order):
    groups = []
    for p in range(4):
        for part in (mine, theirs):
            groups.append(lax.dynamic_index_in_dim(part, p ^ order, 0, keepdims=False))
    return jnp.concatenate(groups, axis=0)


def chunks_of(tiles, cuts):
    ends = [0] + [(tiles * c + 6) // 13 for c in cuts]
    return [(a, b - a) for a, b in zip(ends[:-1], ends[1:])]


def local_tiled(tokens, out_grad, gate_weight, up_weight, down_weight, gate_mask, up_mask, down_mask):
    order = lax.axis_index("row") ^ (lax.axis_index("col") // 2)
    tiles = gate_weight.shape[1] // TILE
    gate_up_bits = pack_gate_up(gate_mask, up_mask)
    tok_mine, gate_up_bits = lax.optimization_barrier((gather_groups(tokens), gate_up_bits))
    tok_mine = jnp.stack(tok_mine)
    tok_theirs = _col_swap(tok_mine, 1)
    tok = order_groups(tok_mine, tok_theirs, order)
    gate_up = lambda c, after: gate_up_sums(tok, gate_weight, up_weight, gate_up_bits, *c, after=after)
    back = lambda c, after: back_sums(grads, down_weight, down_bits, *c, after=after)
    gate_up_red, back_red = Reduction(), [Reduction(), Reduction()]

    cuts = chunks_of(tiles, GATE_UP_CUTS)
    sums0 = gate_up(cuts[0], [])
    gate_up_red.first(sums0)
    sums1 = gate_up(cuts[1], [sums0[0]])
    gate_up_red.hold_first(sums1[0])
    gate_up_red.first(sums1)
    grad_mine = gather_groups(_hold(out_grad, sums1[0]))
    down_bits = pack_down(down_mask, [sums1[0], *gate_up_red.received[0]])
    gate_up_red.hold_first(down_bits)
    grad_mine = jnp.stack(_hold(grad_mine, down_bits))
    grad_theirs = _col_swap(grad_mine, 1)
    gate_up_red.mixed()
    gate_up_red.second()
    grads = order_groups(grad_mine, grad_theirs, order)
    cuts = chunks_of(tiles, BACK_CUTS)
    sums0 = back(cuts[0], [gate_up_red.mixed_x, gate_up_red.mixed_y])
    back_red[0].first(sums0)
    sums1 = back(cuts[1], [sums0[0]])
    back_red[0].hold_first(sums1[0])
    sums1 = _hold(sums1, back_red[0].received[0])
    gate_up_red.hold_second(sums1[0])
    back_red[0].mixed()
    back_red[0].second()
    back_red[1].first(sums1)
    gate_up_total = gate_up_red.total()
    hidden = Gathering(swiglu(*gate_up_total)[None])
    gate_up_total = _hold(gate_up_total, hidden.block)
    split = cuts[1][0] * TILE
    gath = [Gathering(swiglu_back(*gate_up_total[:, :, :split], *back_red[0].total()))]
    gath[0].first()
    back_red[1].hold_first(gath[0].block)
    back_red[1].mixed()
    back_red[1].second()
    gath[0].hold_first(back_red[1].mixed_x)
    gath[0].cut()
    gath[0].second()
    gath.append(Gathering(swiglu_back(*gate_up_total[:, :, split:], *back_red[1].total())))
    gath[1].first()
    pair = (gate_weight, up_weight)
    acc = backward(gath[0].blocks, gate_up_bits, *cuts[0], inputs=(*pair, None), after=[gath[1].block])
    gath[1].hold_first(acc[0])
    gath[1].cut()
    gath[1].second()
    hidden.block = _hold(hidden.block, gath[1].blocks[3:])
    hidden.first()
    outs = backward(gath[0].blocks, gate_up_bits, *cuts[0], weights=(tok, None), after=[gath[1].cut_x, gath[1].cut_y])
    acc = backward(gath[1].blocks, gate_up_bits, *cuts[1], inputs=(*pair, acc), after=[outs[0]])
    hidden.hold_first(acc[0])
    hidden.cut()
    acc = _hold(acc, (hidden.cut_x, hidden.cut_y))
    hidden.second()
    pairs = acc[0] + _col_swap(acc[1], 1)
    own = lax.dynamic_index_in_dim(pairs, order, 0, keepdims=False)
    sent = [lax.dynamic_index_in_dim(pairs, k ^ order, 0, keepdims=False).astype(BF16) for k in (1, 2, 3)]
    received = [_col_swap(value, 2 * k) for k, value in zip((1, 2, 3), sent)]
    outs = backward(gath[1].blocks, gate_up_bits, *cuts[1], weights=(tok, outs), after=sent)
    down_out = down_grad(hidden.blocks, grads, down_bits, [outs[0]])
    for value in received:
        own = own + value
    return (own.astype(BF16), *outs, down_out)


def tiled_fits(mesh, depth, width, token_rows):
    return (
        mesh.shape["row"] == 4
        and mesh.shape["col"] == 8
        and depth % 1280 == 0
        and depth // 512 <= 7
        and depth % 512 == 0
        and width % TILE == 0
        and width // TILE >= 13
        and token_rows % 256 == 0
    )


def solution(mesh):
    in_specs = (
        P("col", "row"),
        P("col", "row"),
        P("row", "col"),
        P("row", "col"),
        P("col", "row"),
        P("row", "col"),
        P("row", "col"),
        P("col", "row"),
    )
    out_specs = (P("col", "row"), P("row", "col"), P("row", "col"), P("col", "row"))

    def run(tokens, out_grad, gate_weight, *rest):
        depth = gate_weight.shape[0] // mesh.shape["row"]
        width = gate_weight.shape[1] // mesh.shape["col"]
        body = local_tiled if tiled_fits(mesh, depth, width, tokens.shape[0]) else local_any
        mapped = jax.shard_map(body, mesh=mesh, in_specs=in_specs, out_specs=out_specs, check_vma=False)
        return mapped(tokens, out_grad, gate_weight, *rest)

    return run
```
